32 devices in a mesh: sp: 8 (over y, x, core), dp: 4 (over z).
Axes of the slice: x: 2, y: 2, z: 4, core: 2. Of those that a mesh axis runs over, the one named last changes fastest.
Arguments:
- hidden: bfloat16 [4, 2048, 4096], P('dp', 'sp'), may hold values from -24 to 24
- pad_counts: int32 [4, 8], P('dp', 'sp'), may hold values from 64 to 128
- doc_lengths: int32 [4, 32], P('dp'), may hold values from 1 to 128, 2048 in all within a row
- range_shift: int32 [4, 8], P('dp'), may hold values from -32 to 32
- qkv_weight: bfloat16 [4096, 384], P('dp'), may hold values from -0.09375 to 0.09375
Outputs:
- attended: bfloat16 [4, 2048, 128], P('dp', 'sp')
The draws below stay inside these ranges and needn't reach their ends.
Inputs may be any that keep to these rules, and one draw needn't show every extreme that they name: `doc_lengths`: each row sums to 2048.
All inputs are finite; a program needn't handle non-finite values.
Results may differ from the reference program's by a relative error of at most 0.0095.
Values may be sent and summed in bfloat16 or wider, within the bound.
A program may use at most 64 MiB of HBM per device.

```python
import math
import jax
import jax.numpy as jnp
import numpy as np
from jax import lax

D = 4096
HEAD_DIM = 128
ROWS_DEV = 256
MICRO = 4
SLOTS = 2048
DOCS = 32
N_SP = 8
N_DP = 4


def draw_hidden(key, part):
    normal_rows = jnp.clip(jax.random.normal(key, (MICRO, SLOTS, D), jnp.float32), -6.0, 6.0)
    return normal_rows.astype(jnp.bfloat16)


def with_ends(entries, own_key, least, top_value):
    longest = entries.shape.index(max(entries.shape))
    spots = []
    for shift in (0, 1):
        where = [jax.random.randint(jax.random.fold_in(own_key, axis), (), 0, length) for axis, length in enumerate(entries.shape)]
        where[longest] = (where[longest] + shift) % entries.shape[longest]
        spots.append(tuple(where))
    return entries.at[spots[0]].set(least).at[spots[1]].set(top_value)


def levels(stream_key, extent, shards, least, top_value):
    loudness, own = 1.0, jax.random.fold_in(stream_key, 6)
    for axis_at, blocks in shards:
        draws = jnp.exp(jax.random.uniform(jax.random.fold_in(own, axis_at), (blocks,), jnp.float32, least / len(shards), top_value / len(shards)))
        loudness = loudness * jnp.repeat(draws, extent[axis_at] // blocks).reshape([-1 if axis == axis_at else 1 for axis in range(len(extent))])
    return loudness


def split_up(count, total, reach, lean):
    portions = [(1 << 20) // math.isqrt(grade ** lean) + 1 for grade in range(2, count + 1)]
    spare, given = total - reach - (count - 1), [1] * (count - 1)
    while spare > 0:
        movable = [i for i in range(count - 1) if given[i] < reach]
        mass, remaining = sum([portions[i] for i in movable]), spare
        for i in movable:
            more = min(reach - given[i], max(1, remaining * portions[i] // mass), spare)
            given[i] = given[i] + more
            spare = spare - more
    return np.array([reach] + given)


def ragged(own_key, number_of, total, bound, skew):
    if number_of == 2:
        one = jax.random.randint(own_key, (), max(1, total - bound), min(bound, total - 1) + 1)
        return jnp.stack([one, total - one])
    tallies = jnp.asarray(split_up(number_of, total, bound, skew), jnp.int32)
    twos = (number_of - 1) // 2
    donor, receiver = tallies[1:1 + 2 * twos:2], tallies[2:2 + 2 * twos:2]
    margin = jnp.minimum(donor - 1, bound - receiver)
    shifted = jax.random.randint(jax.random.fold_in(own_key, 1), (twos,), 0, 1 << 20) % (margin + 1)
    tallies = tallies.at[1:1 + 2 * twos:2].set(donor - shifted).at[2:2 + 2 * twos:2].set(receiver + shifted)
    return tallies[jax.random.permutation(jax.random.fold_in(own_key, 2), number_of)]


def centred(key, shape, deviation, most, cuts=(), kind=jnp.bfloat16):
    array = jax.random.normal(key, shape, jnp.float32) * deviation
    if len(cuts) > 0:
        array = levels(key, shape, cuts, -0.22, 0.18) * array
    return jnp.clip(array, min=-most, max=most).astype(kind)


def setup_inputs(seed: int = 0) -> dict:
    seeds = jax.random.split(jax.random.key(seed), 6)
    return {
        "hidden": draw_hidden(jax.random.fold_in(seeds[5], 71), 0),
        "pad_counts": with_ends(jax.random.randint(seeds[1], (MICRO, N_SP), ROWS_DEV // 4, ROWS_DEV // 2 + 1), jax.random.fold_in(seeds[1], 1), ROWS_DEV // 4, (ROWS_DEV // 2 + 1) - 1).astype(jnp.int32),
        "doc_lengths": jax.vmap(lambda own: ragged(own, DOCS, SLOTS, ROWS_DEV // 2, 1))(jax.random.split(seeds[2], MICRO)).reshape((MICRO, DOCS)).astype(jnp.int32),
        "range_shift": with_ends(jax.random.randint(seeds[3], (MICRO, N_SP), 0 - ROWS_DEV // 8, ROWS_DEV // 8 + 1), jax.random.fold_in(seeds[3], 1), 0 - ROWS_DEV // 8, (ROWS_DEV // 8 + 1) - 1).astype(jnp.int32),
        "qkv_weight": centred(seeds[4], (D, 3 * HEAD_DIM), D ** -0.5, 0.09375, ((0, 4),)),
    }


def attend_block(projected, position, row_live, doc_ids):
    head_dim = projected.shape[1] // 3
    query = projected[:, :head_dim].astype(jnp.float32)
    keys = projected[:, head_dim:2 * head_dim].astype(jnp.float32)
    values = projected[:, 2 * head_dim:].astype(jnp.float32)
    scores = jnp.einsum('qd,kd->qk', query, keys) / math.sqrt(head_dim)
    allowed = (doc_ids[:, None] == doc_ids[None, :]) & (position[None, :] <= position[:, None])
    allowed = allowed & row_live[:, None] & row_live[None, :]
    masked = jnp.where(allowed, scores, -1e+30)
    row_peak = lax.optimization_barrier(jnp.max(masked, axis=1, keepdims=True))
    exponent = jnp.where(allowed, jnp.exp(masked - row_peak), 0.0)
    denominator = lax.optimization_barrier(jnp.sum(exponent, axis=1, keepdims=True))
    attention_probs = (exponent / jnp.where(row_live[:, None], denominator, 1.0)).astype(jnp.bfloat16)
    result = jnp.einsum('qk,kd->qd', attention_probs.astype(jnp.float32), values)
    return jnp.where(row_live[:, None], result, 0.0).astype(jnp.bfloat16)

def reference(hidden, pad_counts, doc_lengths, range_shift, qkv_weight):

    def one_micro(operands):
        slot_rows, padding, lengths, shifts = operands
        live_count = (ROWS_DEV - padding).astype(jnp.int32)
        token_start = (jnp.cumsum(live_count) - live_count).astype(jnp.int32)
        total_tokens = (token_start[-1] + live_count[-1]).astype(jnp.int32)
        range_first = jnp.concatenate([jnp.zeros((1,), jnp.int32), (token_start[1:] + shifts[1:]).astype(jnp.int32)])
        range_end = jnp.concatenate([range_first[1:], total_tokens[None]]).astype(jnp.int32)
        local_rows = jnp.arange(ROWS_DEV, dtype=jnp.int32)
        position = (range_first[:, None] + local_rows[None, :]).astype(jnp.int32)
        row_live = local_rows[None, :] < (range_end - range_first)[:, None]
        device_of = (lax.optimization_barrier(jnp.sum((token_start[None, None, :] <= position[:, :, None]).astype(jnp.int32), axis=2)) - 1).astype(jnp.int32)
        slot_of = (jnp.take(padding, device_of) + position - jnp.take(token_start, device_of)).astype(jnp.int32)
        flat_slot = jnp.clip(device_of * ROWS_DEV + slot_of, 0, N_SP * ROWS_DEV - 1).astype(jnp.int32)
        gathered = jnp.take(slot_rows, flat_slot.reshape(-1), axis=0).reshape(N_SP, ROWS_DEV, D)
        owned_rows = jnp.where(row_live[:, :, None], gathered, 0).astype(jnp.bfloat16)
        projected = jnp.dot(owned_rows.reshape(N_SP * ROWS_DEV, D), qkv_weight, preferred_element_type=jnp.float32)
        projected = projected.astype(jnp.bfloat16).reshape(N_SP, ROWS_DEV, 3 * HEAD_DIM)
        doc_ends = jnp.cumsum(lengths).astype(jnp.int32)
        doc_ids = lax.optimization_barrier(jnp.sum((doc_ends[None, None, :] <= position[:, :, None]).astype(jnp.int32), axis=2)).astype(jnp.int32)
        return jax.vmap(attend_block)(projected, position, row_live, doc_ids)
    blocks = lax.map(one_micro, (hidden, pad_counts, doc_lengths, range_shift))
    return blocks.reshape(N_DP, N_SP * ROWS_DEV, HEAD_DIM)
```

```python
import functools
import math

import jax
import jax.numpy as jnp
from jax import lax
from jax.experimental import pallas as pl
from jax.experimental.pallas import tpu as pltpu
from jax.sharding import PartitionSpec as P

MESH = pl.DeviceIdType.MESH


def flipped(index, bits):
    out, bit = index, 1
    while bit <= bits:
        if bits & bit:
            out = out + bit - 2 * bit * ((index // bit) % 2)
        bit *= 2
    return out


def share_count(chips, depth):
    for shares in (4, 2):
        halves = 2 if shares == 4 else 1
        if chips % shares == 0 and depth % (2 * shares * halves * 16) == 0:
            return shares
    return 1


def kernel(
    n_sp,
    n_dp,
    shares,
    hidden_ref,
    pad_ref,
    docs_ref,
    shift_ref,
    weight_ref,
    out_ref,
    rows_buf,
    weights,
    total,
    pads,
    cand,
    head,
    local_sem,
    z_send,
    z_recv,
    plane_send,
    plane_recv,
    diag_send,
    diag_recv,
    sib_send,
    sib_recv,
    pad_send,
    pad_recv,
    edge_send,
    edge_recv,
):
    sp, dp = lax.axis_index("sp"), lax.axis_index("dp")
    rows_dev = hidden_ref.shape[1]
    depth, columns = weight_ref.shape
    head_dim = columns // 3
    least_pad = rows_dev // 4
    slots = rows_dev - least_pad
    edge = rows_dev // 8
    core = sp % 2
    place = (sp // 2) % shares
    sibling = flipped(sp, 1)
    piece = depth // (2 * shares)
    over_x, over_y, over_xy = flipped(place, 1), flipped(place, 2), flipped(place, 3)
    x_peer, y_peer = flipped(sp, 2), flipped(sp, 4)
    shards = [flipped(dp, j) for j in range(1, n_dp)]
    prior, later = (sp + n_sp - 1) % n_sp, (sp + 1) % n_sp

    def rows_of(which_core, which_place, half=None):
        start = (which_core * shares + which_place) * piece
        if half is None:
            return pl.ds(pl.multiple_of(start, 16), piece)
        return pl.ds(pl.multiple_of(start + half * (piece // 2), 16), piece // 2)

    fetch_rows = pltpu.make_async_copy(
        hidden_ref.at[0, pl.ds(least_pad, slots), :], rows_buf, local_sem.at[0]
    )
    fetch_rows.start()
    fetch_weight = pltpu.make_async_copy(weight_ref, weights.at[dp], local_sem.at[1])
    fetch_weight.start()
    padding = pad_ref[0, 0]
    pads[sp] = jnp.full(pads.shape[1:], padding, jnp.int32)

    barrier = pltpu.get_barrier_semaphore()
    for j in range(1, n_sp):
        pl.semaphore_signal(
            barrier, inc=1, device_id={"sp": (sp + j) % n_sp}, device_id_type=MESH
        )
    for j in range(1, n_dp):
        pl.semaphore_signal(
            barrier, inc=1, device_id={"dp": shards[j - 1]}, device_id_type=MESH
        )
    pl.semaphore_wait(barrier, n_sp - 1 + n_dp - 1)

    started = []

    def send(src, dst, send_sem, recv_sem, device):
        copy = pltpu.make_async_remote_copy(
            src_ref=src,
            dst_ref=dst,
            send_sem=send_sem,
            recv_sem=recv_sem,
            device_id=device,
            device_id_type=MESH,
        )
        copy.start()
        started.append(copy)

    def arrived(dst, send_sem, recv_sem, device):
        pltpu.make_async_remote_copy(
            src_ref=dst,
            dst_ref=dst,
            send_sem=send_sem,
            recv_sem=recv_sem,
            device_id=device,
            device_id_type=MESH,
        ).wait_recv()

    own = rows_of(core, place)
    for j in range(n_dp - 1):
        send(
            weight_ref.at[own, :],
            weights.at[dp, own, :],
            z_send.at[j],
            z_recv.at[j],
            {"dp": shards[j]},
        )
    for j in range(1, n_sp):
        send(pads.at[sp], pads.at[sp], pad_send.at[j - 1], pad_recv.at[j - 1], {"sp": (sp + j) % n_sp})

    def to_sibling(j, slot, rows):
        block = weights.at[shards[j], rows, :]
        send(block, block, sib_send.at[j, slot], sib_recv.at[j, slot], {"sp": sibling})

    def from_plane(j):
        block = weights.at[shards[j], own, :]
        arrived(block, z_send.at[j], z_recv.at[j], {"dp": shards[j]})
        if shares >= 2:
            send(block, block, plane_send.at[j, 0], plane_recv.at[j, 0], {"sp": x_peer})
        if shares >= 4:
            send(block, block, plane_send.at[j, 1], plane_recv.at[j, 1], {"sp": y_peer})
        to_sibling(j, 0, own)

    def from_neighbours(j):
        if shares >= 2:
            rows = rows_of(core, over_x)
            arrived(weights.at[shards[j], rows, :], plane_send.at[j, 0], plane_recv.at[j, 0], {"sp": x_peer})
            if shares >= 4:
                block = weights.at[shards[j], rows_of(core, over_x, 0), :]
                send(block, block, diag_send.at[j, 0], diag_recv.at[j, 0], {"sp": y_peer})
            to_sibling(j, 1, rows)
        if shares >= 4:
            rows = rows_of(core, over_y)
            arrived(weights.at[shards[j], rows, :], plane_send.at[j, 1], plane_recv.at[j, 1], {"sp": y_peer})
            block = weights.at[shards[j], rows_of(core, over_y, 1), :]
            send(block, block, diag_send.at[j, 1], diag_recv.at[j, 1], {"sp": x_peer})
            to_sibling(j, 2, rows)

    def from_diagonal(j):
        if shares >= 4:
            for half, peer in ((0, y_peer), (1, x_peer)):
                block = weights.at[shards[j], rows_of(core, over_xy, half), :]
                arrived(block, diag_send.at[j, half], diag_recv.at[j, half], {"sp": peer})
            to_sibling(j, 3, rows_of(core, over_xy))

    def from_sibling(j):
        places = [place, over_x, over_y, over_xy][:shares]
        for slot, which in enumerate(places):
            block = weights.at[shards[j], rows_of(1 - core, which), :]
            arrived(block, sib_send.at[j, slot], sib_recv.at[j, slot], {"sp": sibling})

    def product(shard):
        part = pl.ds(pl.multiple_of(shard * depth, 128), depth)
        return jnp.dot(rows_buf[:, part], weights[shard], preferred_element_type=jnp.float32)

    def own_shard():
        fetch_rows.wait()
        fetch_weight.wait()
        total[...] = product(dp)

    own_shard()
    for j in range(n_dp - 1):
        from_plane(j)
        if j > 0:
            from_diagonal(j - 1)
        from_neighbours(j)
        if j > 0:
            from_sibling(j - 1)
            total[...] += product(shards[j - 1])

    for j in range(1, n_sp):
        block = pads.at[(sp + n_sp - j) % n_sp]
        arrived(block, pad_send.at[j - 1], pad_recv.at[j - 1], {"sp": (sp + j) % n_sp})
    before = jnp.zeros(pads.shape[1:], jnp.int32)
    for i in range(n_sp):
        before = before + jnp.where(i < sp, rows_dev - pads[i], 0)
    live = rows_dev - padding
    shift = jnp.where(sp == 0, 0, shift_ref[0, sp])
    next_shift = jnp.where(sp == n_sp - 1, 0, shift_ref[0, later])
    owned_count = live + next_shift - shift
    docs = docs_ref.shape[1]
    lengths = jnp.broadcast_to(docs_ref[...].astype(jnp.float32), (8, docs)).astype(jnp.bfloat16)
    upper = (
        lax.broadcasted_iota(jnp.int32, (docs, docs), 0)
        <= lax.broadcasted_iota(jnp.int32, (docs, docs), 1)
    ).astype(jnp.float32).astype(jnp.bfloat16)
    ends = jnp.dot(lengths, upper, preferred_element_type=jnp.float32)[0:1].astype(jnp.int32)
    row = lax.broadcasted_iota(jnp.int32, (rows_dev, rows_dev), 0)
    col = lax.broadcasted_iota(jnp.int32, (rows_dev, rows_dev), 1)
    doc_row = lax.broadcasted_iota(jnp.int32, (rows_dev, docs), 0)
    local_ends = jnp.broadcast_to(ends - before[0:1, 0:1] - shift, (rows_dev, docs))
    doc_start = jnp.max(
        jnp.where(local_ends <= doc_row, local_ends, -(before[0:1, 0:1] + shift)).astype(jnp.float32),
        axis=1,
        keepdims=True,
    )
    allowed = (col <= row) & (col.astype(jnp.float32) >= doc_start)
    moved = row + shift
    target = jnp.where(
        moved < 0, edge + moved, jnp.where(moved < live, padding + moved, edge + moved - live)
    )
    pick = ((col == target) & (row < owned_count)).astype(jnp.float32).astype(jnp.bfloat16)
    head_row = lax.broadcasted_iota(jnp.int32, (edge, slots), 0)
    head_col = lax.broadcasted_iota(jnp.int32, (edge, slots), 1)
    head_pick = (head_col == head_row + padding - least_pad).astype(jnp.float32).astype(jnp.bfloat16)
    query_live = lax.broadcasted_iota(jnp.int32, (rows_dev, head_dim), 0) < owned_count

    if n_dp > 1:
        from_diagonal(n_dp - 2)
        from_sibling(n_dp - 2)
        projected = (total[...] + product(shards[n_dp - 2])).astype(jnp.bfloat16)
    else:
        projected = total[...].astype(jnp.bfloat16)

    own_rows = pl.ds(2 * edge, slots)
    cand[own_rows, :] = projected
    tail = cand.at[pl.ds(rows_dev - edge, edge), :]
    send(tail, cand.at[pl.ds(0, edge), :], edge_send.at[0], edge_recv.at[0], {"sp": later})
    head[...] = jnp.dot(head_pick, projected, preferred_element_type=jnp.float32).astype(jnp.bfloat16)
    send(head, cand.at[pl.ds(edge, edge), :], edge_send.at[1], edge_recv.at[1], {"sp": prior})
    arrived(cand.at[pl.ds(0, edge), :], edge_send.at[0], edge_recv.at[0], {"sp": later})
    arrived(cand.at[pl.ds(edge, edge), :], edge_send.at[1], edge_recv.at[1], {"sp": prior})

    qkv = jnp.dot(pick, cand[...], preferred_element_type=jnp.float32).astype(jnp.bfloat16)
    query, keys, values = qkv[:, :head_dim], qkv[:, head_dim : 2 * head_dim], qkv[:, 2 * head_dim :]
    scores = lax.dot_general(
        query, keys, (((1,), (1,)), ((), ())), preferred_element_type=jnp.float32
    ) * (1.0 / math.sqrt(head_dim))
    masked = jnp.where(allowed, scores, -1e30)
    peak = jnp.max(masked, axis=1, keepdims=True)
    exponent = jnp.where(allowed, jnp.exp(masked - peak), 0.0)
    probs = (exponent / jnp.sum(exponent, axis=1, keepdims=True)).astype(jnp.bfloat16)
    result = jnp.dot(probs, values, preferred_element_type=jnp.float32)
    out_ref[0] = jnp.where(query_live, result, 0.0).astype(out_ref.dtype)
    for copy in started:
        copy.wait_send()


def solution(mesh):
    n_sp, n_dp = mesh.shape["sp"], mesh.shape["dp"]

    def step(hidden, pad_counts, doc_lengths, range_shift, qkv_weight):
        rows_dev, width = hidden.shape[1:]
        depth, columns = qkv_weight.shape
        shares = share_count(n_sp // 2, depth)
        edge, slots = rows_dev // 8, rows_dev - rows_dev // 4
        others = max(n_dp - 1, 1)
        dma = pltpu.SemaphoreType.DMA
        return pl.pallas_call(
            functools.partial(kernel, n_sp, n_dp, shares),
            out_shape=jax.ShapeDtypeStruct((1, rows_dev, columns // 3), hidden.dtype),
            in_specs=[
                pl.BlockSpec(memory_space=pl.ANY),
                pl.BlockSpec(memory_space=pltpu.SMEM),
                pl.BlockSpec(memory_space=pltpu.VMEM),
                pl.BlockSpec(memory_space=pltpu.SMEM),
                pl.BlockSpec(memory_space=pl.ANY),
            ],
            out_specs=pl.BlockSpec(memory_space=pltpu.VMEM),
            scratch_shapes=[
                pltpu.VMEM((slots, width), hidden.dtype),
                pltpu.VMEM((n_dp, depth, columns), qkv_weight.dtype),
                pltpu.VMEM((slots, columns), jnp.float32),
                pltpu.VMEM((n_sp, 8, 128), jnp.int32),
                pltpu.VMEM((rows_dev, columns), hidden.dtype),
                pltpu.VMEM((edge, columns), hidden.dtype),
                dma((2,)),
                dma((others,)),
                dma((others,)),
                dma((others, 2)),
                dma((others, 2)),
                dma((others, 2)),
                dma((others, 2)),
                dma((others, shares)),
                dma((others, shares)),
                dma((n_sp - 1,)),
                dma((n_sp - 1,)),
                dma((2,)),
                dma((2,)),
            ],
            compiler_params=pltpu.CompilerParams(
                collective_id=0, has_side_effects=True, vmem_limit_bytes=48 * 1024 * 1024
            ),
            cost_estimate=pl.CostEstimate(
                flops=2 * slots * width * columns,
                bytes_accessed=2 * width * (rows_dev + columns),
                transcendentals=rows_dev * rows_dev,
            ),
        )(hidden, pad_counts, doc_lengths, range_shift, qkv_weight)

    in_specs = (P("dp", "sp", None), P("dp", "sp"), P("dp", None), P("dp", None), P("dp", None))
    return jax.shard_map(
        step, mesh=mesh, in_specs=in_specs, out_specs=P("dp", "sp", None), check_vma=False
    )
```

```python
import functools
import math

import jax
import jax.numpy as jnp
from jax import lax
from jax.experimental import pallas as pl
from jax.experimental.pallas import tpu as pltpu
from jax.sharding import PartitionSpec as P

MESH = pl.DeviceIdType.MESH


def flipped(index, bits):
    out, bit = index, 1
    while bit <= bits:
        if bits & bit:
            out = out + bit - 2 * bit * ((index // bit) % 2)
        bit *= 2
    return out


def flipped(index, bits):
    out, bit = index, 1
    while bit <= bits:
        if bits & bit:
            out = out + bit - 2 * bit * ((index // bit) % 2)
        bit *= 2
    return out


def nearest_first(index, count):
    both = jnp.minimum(index, count - 1 - index)
    longer = jnp.where(index <= count - 1 - index, 1, -1)
    out = []
    for j in range(1, count):
        near = (j + 1) // 2 if j % 2 else -(j // 2)
        out.append(index + jnp.where(j <= 2 * both, near, longer * (j - both)))
    return out


def share_count(chips, depth):
    for shares in (4, 2):
        halves = 2 if shares == 4 else 1
        if chips % shares == 0 and depth % (2 * shares * halves * 16) == 0:
            return shares
    return 1


def kernel(
    n_sp,
    n_dp,
    shares,
    hidden_ref,
    pad_hbm,
    docs_hbm,
    shift_hbm,
    weight_ref,
    out_ref,
    pad_ref,
    docs_ref,
    shift_ref,
    rows_buf,
    weights,
    total,
    pads,
    cand,
    head,
    local_sem,
    z_send,
    z_recv,
    plane_send,
    plane_recv,
    diag_send,
    diag_recv,
    sib_send,
    sib_recv,
    pad_send,
    pad_recv,
    edge_send,
    edge_recv,
):
    sp, dp = lax.axis_index("sp"), lax.axis_index("dp")
    rows_dev = hidden_ref.shape[1]
    depth, columns = weight_ref.shape
    head_dim = columns // 3
    least_pad = rows_dev // 4
    slots = rows_dev - least_pad
    edge = rows_dev // 8
    core = sp % 2
    place = (sp // 2) % shares
    sibling = flipped(sp, 1)
    piece = depth // (2 * shares)
    over_x, over_y, over_xy = flipped(place, 1), flipped(place, 2), flipped(place, 3)
    x_peer, y_peer = flipped(sp, 2), flipped(sp, 4)
    shards = nearest_first(dp, n_dp)
    inner = (dp > 0) & (dp < n_dp - 1)
    prior, later = (sp + n_sp - 1) % n_sp, (sp + 1) % n_sp

    def rows_of(which_core, which_place, half=None):
        start = (which_core * shares + which_place) * piece
        if half is None:
            return pl.ds(pl.multiple_of(start, 16), piece)
        return pl.ds(pl.multiple_of(start + half * (piece // 2), 16), piece // 2)

    fetch_rows = pltpu.make_async_copy(
        hidden_ref.at[0, pl.ds(least_pad, slots), :], rows_buf, local_sem.at[0]
    )
    fetch_rows.start()
    fetch_weight = pltpu.make_async_copy(weight_ref, weights.at[dp], local_sem.at[1])
    fetch_weight.start()
    fetch_pad = pltpu.make_async_copy(pad_hbm, pad_ref, local_sem.at[2])
    fetch_pad.start()
    fetch_docs = pltpu.make_async_copy(docs_hbm, docs_ref, local_sem.at[3])
    fetch_docs.start()
    fetch_shift = pltpu.make_async_copy(shift_hbm, shift_ref, local_sem.at[4])
    fetch_shift.start()

    barrier = pltpu.get_barrier_semaphore()
    for j in range(1, n_sp):
        pl.semaphore_signal(
            barrier, inc=1, device_id={"sp": (sp + j) % n_sp}, device_id_type=MESH
        )
    for j in range(1, n_dp):
        pl.semaphore_signal(
            barrier, inc=1, device_id={"dp": (dp + j) % n_dp}, device_id_type=MESH
        )
    pl.semaphore_wait(barrier, n_sp - 1 + n_dp - 1)

    started = []

    def send(src, dst, send_sem, recv_sem, device, when=None):
        def copy():
            return pltpu.make_async_remote_copy(
                src_ref=src(),
                dst_ref=dst(),
                send_sem=send_sem,
                recv_sem=recv_sem,
                device_id=device,
                device_id_type=MESH,
            )

        if when is None:
            copy().start()
        else:
            pl.when(when)(lambda: copy().start())
        started.append((copy, when))

    def arrived(dst, send_sem, recv_sem, device):
        pltpu.make_async_remote_copy(
            src_ref=dst,
            dst_ref=dst,
            send_sem=send_sem,
            recv_sem=recv_sem,
            device_id=device,
            device_id_type=MESH,
        ).wait_recv()

    own = rows_of(core, place)
    own_source = lambda: weight_ref.at[own, :]
    own_target = lambda: weights.at[dp, own, :]
    if n_dp > 1:
        send(own_source, own_target, z_send.at[n_dp], z_recv.at[dp], {"dp": dp + 1}, when=dp < n_dp - 1)
        send(own_source, own_target, z_send.at[n_dp + 1], z_recv.at[dp], {"dp": dp - 1}, when=dp > 0)
    fetch_pad.wait()
    padding = pad_ref[0, 0]
    pads[sp] = jnp.full(pads.shape[1:], padding, jnp.int32)
    for j in range(1, n_sp):
        block = lambda: pads.at[sp]
        send(block, block, pad_send.at[j - 1], pad_recv.at[j - 1], {"sp": (sp + j) % n_sp})

    def to_sibling(j, slot, rows):
        block = lambda: weights.at[shards[j], rows, :]
        send(block, block, sib_send.at[j, slot], sib_recv.at[j, slot], {"sp": sibling})

    def piece_copies(j):
        shard = shards[j]
        onward = jnp.where(shard < dp, dp + 1, dp - 1)
        block = weights.at[shard, own, :]
        ways = [
            (z_send.at[shard], z_recv.at[shard], {"dp": onward}, (onward >= 0) & (onward < n_dp))
        ]
        if shares >= 2:
            ways.append((plane_send.at[j, 0], plane_recv.at[j, 0], {"sp": x_peer}, None))
        if shares >= 4:
            ways.append((plane_send.at[j, 1], plane_recv.at[j, 1], {"sp": y_peer}, None))
        ways.append((sib_send.at[j, 0], sib_recv.at[j, 0], {"sp": sibling}, None))
        return [
            (
                lambda ways=(out, into, peer): pltpu.make_async_remote_copy(
                    src_ref=block,
                    dst_ref=block,
                    send_sem=ways[0],
                    recv_sem=ways[1],
                    device_id=ways[2],
                    device_id_type=MESH,
                ),
                when,
            )
            for out, into, peer, when in ways
        ]

    def from_plane(j):
        shard = shards[j]
        origin = jnp.where(shard < dp, dp - 1, dp + 1)
        arrived(weights.at[shard, own, :], z_send.at[shard], z_recv.at[shard], {"dp": origin})
        for copy, when in piece_copies(j):
            if when is None:
                copy().start()
            else:
                pl.when(when)(lambda: copy().start())

    def from_neighbours(j):
        if shares >= 2:
            rows = rows_of(core, over_x)
            arrived(weights.at[shards[j], rows, :], plane_send.at[j, 0], plane_recv.at[j, 0], {"sp": x_peer})
            if shares >= 4:
                block = lambda: weights.at[shards[j], rows_of(core, over_x, 0), :]
                send(block, block, diag_send.at[j, 0], diag_recv.at[j, 0], {"sp": y_peer})
            to_sibling(j, 1, rows)
        if shares >= 4:
            rows = rows_of(core, over_y)
            arrived(weights.at[shards[j], rows, :], plane_send.at[j, 1], plane_recv.at[j, 1], {"sp": y_peer})
            block = lambda: weights.at[shards[j], rows_of(core, over_y, 1), :]
            send(block, block, diag_send.at[j, 1], diag_recv.at[j, 1], {"sp": x_peer})
            to_sibling(j, 2, rows)

    def from_diagonal(j):
        if shares >= 4:
            for half, peer in ((0, y_peer), (1, x_peer)):
                block = weights.at[shards[j], rows_of(core, over_xy, half), :]
                arrived(block, diag_send.at[j, half], diag_recv.at[j, half], {"sp": peer})
            to_sibling(j, 3, rows_of(core, over_xy))

    def from_sibling(j):
        places = [place, over_x, over_y, over_xy][:shares]
        for slot, which in enumerate(places):
            block = weights.at[shards[j], rows_of(1 - core, which), :]
            arrived(block, sib_send.at[j, slot], sib_recv.at[j, slot], {"sp": sibling})

    def product(shard):
        part = pl.ds(pl.multiple_of(shard * depth, 128), depth)
        return jnp.dot(rows_buf[:, part], weights[shard], preferred_element_type=jnp.float32)

    def own_shard():
        fetch_rows.wait()
        fetch_weight.wait()
        total[...] = product(dp)

    own_shard()
    if n_dp > 1:
        from_plane(0)
    for j in range(n_dp - 1):
        if j < n_dp - 2:
            pl.when(inner)(functools.partial(from_plane, j + 1))
        from_neighbours(j)
        if j > 0:
            from_diagonal(j - 1)
        if j < n_dp - 2:
            pl.when(~inner)(functools.partial(from_plane, j + 1))
        if j > 0:
            from_sibling(j - 1)
            total[...] += product(shards[j - 1])

    for j in range(1, n_sp):
        block = pads.at[(sp + n_sp - j) % n_sp]
        arrived(block, pad_send.at[j - 1], pad_recv.at[j - 1], {"sp": (sp + j) % n_sp})
    before = jnp.zeros(pads.shape[1:], jnp.int32)
    for i in range(n_sp):
        before = before + jnp.where(i < sp, rows_dev - pads[i], 0)
    live = rows_dev - padding
    fetch_docs.wait()
    fetch_shift.wait()
    shift = jnp.where(sp == 0, 0, shift_ref[0, sp])
    next_shift = jnp.where(sp == n_sp - 1, 0, shift_ref[0, later])
    owned_count = live + next_shift - shift
    docs = docs_ref.shape[1]
    lengths = jnp.broadcast_to(docs_ref[...].astype(jnp.float32), (8, docs)).astype(jnp.bfloat16)
    upper = (
        lax.broadcasted_iota(jnp.int32, (docs, docs), 0)
        <= lax.broadcasted_iota(jnp.int32, (docs, docs), 1)
    ).astype(jnp.float32).astype(jnp.bfloat16)
    ends = jnp.dot(lengths, upper, preferred_element_type=jnp.float32)[0:1].astype(jnp.int32)
    row = lax.broadcasted_iota(jnp.int32, (rows_dev, rows_dev), 0)
    col = lax.broadcasted_iota(jnp.int32, (rows_dev, rows_dev), 1)
    doc_row = lax.broadcasted_iota(jnp.int32, (rows_dev, docs), 0)
    local_ends = jnp.broadcast_to(ends - before[0:1, 0:1] - shift, (rows_dev, docs))
    doc_start = jnp.max(
        jnp.where(local_ends <= doc_row, local_ends, -(before[0:1, 0:1] + shift)).astype(jnp.float32),
        axis=1,
        keepdims=True,
    )
    allowed = (col <= row) & (col.astype(jnp.float32) >= doc_start)
    moved = row + shift
    target = jnp.where(
        moved < 0, edge + moved, jnp.where(moved < live, padding + moved, edge + moved - live)
    )
    pick = ((col == target) & (row < owned_count)).astype(jnp.float32).astype(jnp.bfloat16)
    head_row = lax.broadcasted_iota(jnp.int32, (edge, slots), 0)
    head_col = lax.broadcasted_iota(jnp.int32, (edge, slots), 1)
    head_pick = (head_col == head_row + padding - least_pad).astype(jnp.float32).astype(jnp.bfloat16)
    query_live = lax.broadcasted_iota(jnp.int32, (rows_dev, head_dim), 0) < owned_count

    if n_dp > 1:
        from_diagonal(n_dp - 2)
        from_sibling(n_dp - 2)
        projected = (total[...] + product(shards[n_dp - 2])).astype(jnp.bfloat16)
    else:
        projected = total[...].astype(jnp.bfloat16)

    own_rows = pl.ds(2 * edge, slots)
    cand[own_rows, :] = projected
    tail = cand.at[pl.ds(rows_dev - edge, edge), :]
    send(lambda: tail, lambda: cand.at[pl.ds(0, edge), :], edge_send.at[0], edge_recv.at[0], {"sp": later})
    head[...] = jnp.dot(head_pick, projected, preferred_element_type=jnp.float32).astype(jnp.bfloat16)
    send(lambda: head, lambda: cand.at[pl.ds(edge, edge), :], edge_send.at[1], edge_recv.at[1], {"sp": prior})
    arrived(cand.at[pl.ds(0, edge), :], edge_send.at[0], edge_recv.at[0], {"sp": later})
    arrived(cand.at[pl.ds(edge, edge), :], edge_send.at[1], edge_recv.at[1], {"sp": prior})

    qkv = jnp.dot(pick, cand[...], preferred_element_type=jnp.float32).astype(jnp.bfloat16)
    query, keys, values = qkv[:, :head_dim], qkv[:, head_dim : 2 * head_dim], qkv[:, 2 * head_dim :]
    scores = lax.dot_general(
        query, keys, (((1,), (1,)), ((), ())), preferred_element_type=jnp.float32
    ) * (1.0 / math.sqrt(head_dim))
    masked = jnp.where(allowed, scores, -1e30)
    peak = jnp.max(masked, axis=1, keepdims=True)
    exponent = jnp.where(allowed, jnp.exp(masked - peak), 0.0)
    probs = (exponent / jnp.sum(exponent, axis=1, keepdims=True)).astype(jnp.bfloat16)
    result = jnp.dot(probs, values, preferred_element_type=jnp.float32)
    out_ref[0] = jnp.where(query_live, result, 0.0).astype(out_ref.dtype)
    for j in range(n_dp - 1):
        started.extend(piece_copies(j))
    for copy, when in started:
        if when is None:
            copy().wait_send()
        else:
            pl.when(when)(lambda: copy().wait_send())


def solution(mesh):
    n_sp, n_dp = mesh.shape["sp"], mesh.shape["dp"]

    def step(hidden, pad_counts, doc_lengths, range_shift, qkv_weight):
        rows_dev, width = hidden.shape[1:]
        depth, columns = qkv_weight.shape
        shares = share_count(n_sp // 2, depth)
        edge, slots = rows_dev // 8, rows_dev - rows_dev // 4
        others = max(n_dp - 1, 1)
        dma = pltpu.SemaphoreType.DMA
        return pl.pallas_call(
            functools.partial(kernel, n_sp, n_dp, shares),
            out_shape=jax.ShapeDtypeStruct((1, rows_dev, columns // 3), hidden.dtype),
            in_specs=[
                pl.BlockSpec(memory_space=pltpu.HBM),
            ]
            * 5,
            out_specs=pl.BlockSpec(memory_space=pltpu.VMEM),
            scratch_shapes=[
                pltpu.SMEM(pad_counts.shape, jnp.int32),
                pltpu.VMEM(doc_lengths.shape, jnp.int32),
                pltpu.SMEM(range_shift.shape, jnp.int32),
                pltpu.VMEM((slots, width), hidden.dtype),
                pltpu.VMEM((n_dp, depth, columns), qkv_weight.dtype),
                pltpu.VMEM((slots, columns), jnp.float32),
                pltpu.VMEM((n_sp, 8, 128), jnp.int32),
                pltpu.VMEM((rows_dev, columns), hidden.dtype),
                pltpu.VMEM((edge, columns), hidden.dtype),
                dma((5,)),
                dma((n_dp + 2,)),
                dma((n_dp,)),
                dma((others, 2)),
                dma((others, 2)),
                dma((others, 2)),
                dma((others, 2)),
                dma((others, shares)),
                dma((others, shares)),
                dma((n_sp - 1,)),
                dma((n_sp - 1,)),
                dma((2,)),
                dma((2,)),
            ],
            compiler_params=pltpu.CompilerParams(
                collective_id=0, has_side_effects=True, vmem_limit_bytes=63 * 1024 * 1024
            ),
            cost_estimate=pl.CostEstimate(
                flops=2 * slots * width * columns,
                bytes_accessed=2 * width * (rows_dev + columns),
                transcendentals=rows_dev * rows_dev,
            ),
        )(hidden, pad_counts, doc_lengths, range_shift, qkv_weight)

    in_specs = (P("dp", "sp", None), P("dp", "sp"), P("dp", None), P("dp", None), P("dp", None))
    return jax.shard_map(
        step, mesh=mesh, in_specs=in_specs, out_specs=P("dp", "sp", None), check_vma=False
    )
```

```python
import functools
import math

import jax
import jax.numpy as jnp
from jax import lax
from jax.experimental import pallas as pl
from jax.experimental.pallas import tpu as pltpu
from jax.sharding import PartitionSpec as P

MESH = pl.DeviceIdType.MESH
PARTS = 2


def flipped(index, bits):
    out, bit = index, 1
    while bit <= bits:
        if bits & bit:
            out = out + bit - 2 * bit * ((index // bit) % 2)
        bit *= 2
    return out


def flipped(index, bits):
    out, bit = index, 1
    while bit <= bits:
        if bits & bit:
            out = out + bit - 2 * bit * ((index // bit) % 2)
        bit *= 2
    return out


def nearest_first(index, count):
    both = jnp.minimum(index, count - 1 - index)
    longer = jnp.where(index <= count - 1 - index, 1, -1)
    out = []
    for j in range(1, count):
        near = (j + 1) // 2 if j % 2 else -(j // 2)
        out.append(index + jnp.where(j <= 2 * both, near, longer * (j - both)))
    return out


def travel_order(index, count, parts):
    near = nearest_first(index, count)
    both = jnp.minimum(index, count - 1 - index)
    out = []
    for pair in range(0, count - 1, 2):
        if pair + 1 == count - 1:
            out += [(near[pair], part) for part in range(parts)]
            continue
        two_sided = pair // 2 < both
        for step in range(2 * parts):
            shard = jnp.where(two_sided, near[pair + step % 2], near[pair + step // parts])
            out.append((shard, jnp.where(two_sided, step // 2, step % parts)))
    return out


def share_count(chips, depth):
    for shares in (4, 2):
        halves = 2 if shares == 4 else 1
        if chips % shares == 0 and depth % (2 * shares * halves * 16) == 0:
            return shares
    return 1


def kernel(
    n_sp,
    n_dp,
    shares,
    hidden_ref,
    pad_hbm,
    docs_hbm,
    shift_hbm,
    weight_ref,
    out_ref,
    pad_ref,
    docs_ref,
    shift_ref,
    rows_buf,
    weights,
    total,
    pads,
    cand,
    head,
    local_sem,
    z_send,
    z_recv,
    plane_send,
    plane_recv,
    diag_send,
    diag_recv,
    sib_send,
    sib_recv,
    pad_send,
    pad_recv,
    edge_send,
    edge_recv,
):
    sp, dp = lax.axis_index("sp"), lax.axis_index("dp")
    rows_dev = hidden_ref.shape[1]
    depth, columns = weight_ref.shape
    head_dim = columns // 3
    least_pad = rows_dev // 4
    slots = rows_dev - least_pad
    edge = rows_dev // 8
    core = sp % 2
    place = (sp // 2) % shares
    sibling = flipped(sp, 1)
    part_depth = depth // PARTS
    piece = part_depth // (2 * shares)
    over_x, over_y, over_xy = flipped(place, 1), flipped(place, 2), flipped(place, 3)
    x_peer, y_peer = flipped(sp, 2), flipped(sp, 4)
    units = travel_order(dp, n_dp, PARTS)
    origins = [shard for shard, _ in units]
    shards = [shard * PARTS + part for shard, part in units]
    n_units = len(units)
    inner = (dp > 0) & (dp < n_dp - 1)
    prior, later = (sp + n_sp - 1) % n_sp, (sp + 1) % n_sp

    def rows_of(which_core, which_place, half=None):
        start = (which_core * shares + which_place) * piece
        if half is None:
            return pl.ds(pl.multiple_of(start, 16), piece)
        return pl.ds(pl.multiple_of(start + half * (piece // 2), 16), piece // 2)

    fetch_rows = pltpu.make_async_copy(
        hidden_ref.at[0, pl.ds(least_pad, slots), :], rows_buf, local_sem.at[0]
    )
    fetch_rows.start()
    fetch_weights = [
        pltpu.make_async_copy(
            weight_ref.at[pl.ds(part * part_depth, part_depth), :],
            weights.at[dp * PARTS + part],
            local_sem.at[5 + part],
        )
        for part in range(PARTS)
    ]
    for fetch in fetch_weights:
        fetch.start()
    fetch_pad = pltpu.make_async_copy(pad_hbm, pad_ref, local_sem.at[2])
    fetch_pad.start()
    fetch_docs = pltpu.make_async_copy(docs_hbm, docs_ref, local_sem.at[3])
    fetch_docs.start()
    fetch_shift = pltpu.make_async_copy(shift_hbm, shift_ref, local_sem.at[4])
    fetch_shift.start()

    barrier = pltpu.get_barrier_semaphore()
    for j in range(1, n_sp):
        pl.semaphore_signal(
            barrier, inc=1, device_id={"sp": (sp + j) % n_sp}, device_id_type=MESH
        )
    for j in range(1, n_dp):
        pl.semaphore_signal(
            barrier, inc=1, device_id={"dp": (dp + j) % n_dp}, device_id_type=MESH
        )
    pl.semaphore_wait(barrier, n_sp - 1 + n_dp - 1)

    started = []

    def send(src, dst, send_sem, recv_sem, device, when=None):
        def copy():
            return pltpu.make_async_remote_copy(
                src_ref=src(),
                dst_ref=dst(),
                send_sem=send_sem,
                recv_sem=recv_sem,
                device_id=device,
                device_id_type=MESH,
            )

        if when is None:
            copy().start()
        else:
            pl.when(when)(lambda: copy().start())
        started.append((copy, when))

    def arrived(dst, send_sem, recv_sem, device):
        pltpu.make_async_remote_copy(
            src_ref=dst,
            dst_ref=dst,
            send_sem=send_sem,
            recv_sem=recv_sem,
            device_id=device,
            device_id_type=MESH,
        ).wait_recv()

    own = rows_of(core, place)
    for part in range(PARTS if n_dp > 1 else 0):
        mine = dp * PARTS + part
        start = part * part_depth + (core * shares + place) * piece
        own_source = lambda start=start: weight_ref.at[pl.ds(pl.multiple_of(start, 16), piece), :]
        own_target = lambda mine=mine: weights.at[mine, own, :]
        at = n_dp * PARTS + 2 * part
        send(own_source, own_target, z_send.at[at], z_recv.at[mine], {"dp": dp + 1}, dp < n_dp - 1)
        send(own_source, own_target, z_send.at[at + 1], z_recv.at[mine], {"dp": dp - 1}, dp > 0)
    fetch_pad.wait()
    padding = pad_ref[0, 0]
    pads[sp] = jnp.full(pads.shape[1:], padding, jnp.int32)
    for j in range(1, n_sp):
        block = lambda: pads.at[sp]
        send(block, block, pad_send.at[j - 1], pad_recv.at[j - 1], {"sp": (sp + j) % n_sp})

    def to_sibling(j, slot, rows):
        block = lambda: weights.at[shards[j], rows, :]
        send(block, block, sib_send.at[j, slot], sib_recv.at[j, slot], {"sp": sibling})

    def piece_copies(j):
        shard = shards[j]
        onward = jnp.where(origins[j] < dp, dp + 1, dp - 1)
        block = weights.at[shard, own, :]
        ways = [
            (z_send.at[shard], z_recv.at[shard], {"dp": onward}, (onward >= 0) & (onward < n_dp))
        ]
        if shares >= 2:
            ways.append((plane_send.at[j, 0], plane_recv.at[j, 0], {"sp": x_peer}, None))
        if shares >= 4:
            ways.append((plane_send.at[j, 1], plane_recv.at[j, 1], {"sp": y_peer}, None))
        ways.append((sib_send.at[j, 0], sib_recv.at[j, 0], {"sp": sibling}, None))
        return [
            (
                lambda ways=(out, into, peer): pltpu.make_async_remote_copy(
                    src_ref=block,
                    dst_ref=block,
                    send_sem=ways[0],
                    recv_sem=ways[1],
                    device_id=ways[2],
                    device_id_type=MESH,
                ),
                when,
            )
            for out, into, peer, when in ways
        ]

    def from_plane(j):
        shard = shards[j]
        origin = jnp.where(origins[j] < dp, dp - 1, dp + 1)
        arrived(weights.at[shard, own, :], z_send.at[shard], z_recv.at[shard], {"dp": origin})
        for copy, when in piece_copies(j):
            if when is None:
                copy().start()
            else:
                pl.when(when)(lambda: copy().start())

    def from_neighbours(j):
        if shares >= 2:
            rows = rows_of(core, over_x)
            arrived(weights.at[shards[j], rows, :], plane_send.at[j, 0], plane_recv.at[j, 0], {"sp": x_peer})
            if shares >= 4:
                block = lambda: weights.at[shards[j], rows_of(core, over_x, 0), :]
                send(block, block, diag_send.at[j, 0], diag_recv.at[j, 0], {"sp": y_peer})
            to_sibling(j, 1, rows)
        if shares >= 4:
            rows = rows_of(core, over_y)
            arrived(weights.at[shards[j], rows, :], plane_send.at[j, 1], plane_recv.at[j, 1], {"sp": y_peer})
            block = lambda: weights.at[shards[j], rows_of(core, over_y, 1), :]
            send(block, block, diag_send.at[j, 1], diag_recv.at[j, 1], {"sp": x_peer})
            to_sibling(j, 2, rows)

    def from_diagonal(j):
        if shares >= 4:
            for half, peer in ((0, y_peer), (1, x_peer)):
                block = weights.at[shards[j], rows_of(core, over_xy, half), :]
                arrived(block, diag_send.at[j, half], diag_recv.at[j, half], {"sp": peer})
            to_sibling(j, 3, rows_of(core, over_xy))

    def from_sibling(j):
        places = [place, over_x, over_y, over_xy][:shares]
        for slot, which in enumerate(places):
            block = weights.at[shards[j], rows_of(1 - core, which), :]
            arrived(block, sib_send.at[j, slot], sib_recv.at[j, slot], {"sp": sibling})

    def product(unit):
        part = pl.ds(pl.multiple_of(unit * part_depth, 128), part_depth)
        return jnp.dot(rows_buf[:, part], weights[unit], preferred_element_type=jnp.float32)

    fetch_rows.wait()
    for fetch in fetch_weights:
        fetch.wait()
    total[...] = product(dp * PARTS)
    for part in range(1, PARTS):
        total[...] += product(dp * PARTS + part)
    for i in range(4):
        if i < n_units:
            if i < 2:
                from_plane(i)
            else:
                pl.when(inner)(functools.partial(from_plane, i))
    for i in range(n_units):
        from_neighbours(i)
        if i + 4 < n_units:
            pl.when(inner)(functools.partial(from_plane, i + 4))
        if i + 2 < n_units:
            pl.when(~inner)(functools.partial(from_plane, i + 2))
        if i >= 1:
            from_diagonal(i - 1)
        if i >= 2:
            from_sibling(i - 2)
            total[...] += product(shards[i - 2])

    for j in range(1, n_sp):
        block = pads.at[(sp + n_sp - j) % n_sp]
        arrived(block, pad_send.at[j - 1], pad_recv.at[j - 1], {"sp": (sp + j) % n_sp})
    before = jnp.zeros(pads.shape[1:], jnp.int32)
    for i in range(n_sp):
        before = before + jnp.where(i < sp, rows_dev - pads[i], 0)
    live = rows_dev - padding
    fetch_docs.wait()
    fetch_shift.wait()
    shift = jnp.where(sp == 0, 0, shift_ref[0, sp])
    next_shift = jnp.where(sp == n_sp - 1, 0, shift_ref[0, later])
    owned_count = live + next_shift - shift
    docs = docs_ref.shape[1]
    lengths = jnp.broadcast_to(docs_ref[...].astype(jnp.float32), (8, docs)).astype(jnp.bfloat16)
    upper = (
        lax.broadcasted_iota(jnp.int32, (docs, docs), 0)
        <= lax.broadcasted_iota(jnp.int32, (docs, docs), 1)
    ).astype(jnp.float32).astype(jnp.bfloat16)
    ends = jnp.dot(lengths, upper, preferred_element_type=jnp.float32)[0:1].astype(jnp.int32)
    row = lax.broadcasted_iota(jnp.int32, (rows_dev, rows_dev), 0)
    col = lax.broadcasted_iota(jnp.int32, (rows_dev, rows_dev), 1)
    doc_row = lax.broadcasted_iota(jnp.int32, (rows_dev, docs), 0)
    local_ends = jnp.broadcast_to(ends - before[0:1, 0:1] - shift, (rows_dev, docs))
    doc_start = jnp.max(
        jnp.where(local_ends <= doc_row, local_ends, -(before[0:1, 0:1] + shift)).astype(jnp.float32),
        axis=1,
        keepdims=True,
    )
    allowed = (col <= row) & (col.astype(jnp.float32) >= doc_start)
    moved = row + shift
    target = jnp.where(
        moved < 0, edge + moved, jnp.where(moved < live, padding + moved, edge + moved - live)
    )
    pick = ((col == target) & (row < owned_count)).astype(jnp.float32).astype(jnp.bfloat16)
    head_row = lax.broadcasted_iota(jnp.int32, (edge, slots), 0)
    head_col = lax.broadcasted_iota(jnp.int32, (edge, slots), 1)
    head_pick = (head_col == head_row + padding - least_pad).astype(jnp.float32).astype(jnp.bfloat16)
    query_live = lax.broadcasted_iota(jnp.int32, (rows_dev, head_dim), 0) < owned_count

    if n_units:
        from_diagonal(n_units - 1)
        from_sibling(n_units - 2)
        total[...] += product(shards[n_units - 2])
        from_sibling(n_units - 1)
        total[...] += product(shards[n_units - 1])
    projected = total[...].astype(jnp.bfloat16)

    own_rows = pl.ds(2 * edge, slots)
    cand[own_rows, :] = projected
    tail = cand.at[pl.ds(rows_dev - edge, edge), :]
    send(lambda: tail, lambda: cand.at[pl.ds(0, edge), :], edge_send.at[0], edge_recv.at[0], {"sp": later})
    head[...] = jnp.dot(head_pick, projected, preferred_element_type=jnp.float32).astype(jnp.bfloat16)
    send(lambda: head, lambda: cand.at[pl.ds(edge, edge), :], edge_send.at[1], edge_recv.at[1], {"sp": prior})
    arrived(cand.at[pl.ds(0, edge), :], edge_send.at[0], edge_recv.at[0], {"sp": later})
    arrived(cand.at[pl.ds(edge, edge), :], edge_send.at[1], edge_recv.at[1], {"sp": prior})

    qkv = jnp.dot(pick, cand[...], preferred_element_type=jnp.float32).astype(jnp.bfloat16)
    query, keys, values = qkv[:, :head_dim], qkv[:, head_dim : 2 * head_dim], qkv[:, 2 * head_dim :]
    scores = lax.dot_general(
        query, keys, (((1,), (1,)), ((), ())), preferred_element_type=jnp.float32
    ) * (1.0 / math.sqrt(head_dim))
    masked = jnp.where(allowed, scores, -1e30)
    peak = jnp.max(masked, axis=1, keepdims=True)
    exponent = jnp.where(allowed, jnp.exp(masked - peak), 0.0)
    probs = (exponent / jnp.sum(exponent, axis=1, keepdims=True)).astype(jnp.bfloat16)
    result = jnp.dot(probs, values, preferred_element_type=jnp.float32)
    out_ref[0] = jnp.where(query_live, result, 0.0).astype(out_ref.dtype)
    for j in range(n_units):
        started.extend(piece_copies(j))
    for copy, when in started:
        if when is None:
            copy().wait_send()
        else:
            pl.when(when)(lambda: copy().wait_send())


def solution(mesh):
    n_sp, n_dp = mesh.shape["sp"], mesh.shape["dp"]

    def step(hidden, pad_counts, doc_lengths, range_shift, qkv_weight):
        rows_dev, width = hidden.shape[1:]
        depth, columns = qkv_weight.shape
        shares = share_count(n_sp // 2, depth // PARTS)
        edge, slots = rows_dev // 8, rows_dev - rows_dev // 4
        others = max(n_dp - 1, 1) * PARTS
        dma = pltpu.SemaphoreType.DMA
        return pl.pallas_call(
            functools.partial(kernel, n_sp, n_dp, shares),
            out_shape=jax.ShapeDtypeStruct((1, rows_dev, columns // 3), hidden.dtype),
            in_specs=[
                pl.BlockSpec(memory_space=pltpu.HBM),
            ]
            * 5,
            out_specs=pl.BlockSpec(memory_space=pltpu.VMEM),
            scratch_shapes=[
                pltpu.SMEM(pad_counts.shape, jnp.int32),
                pltpu.VMEM(doc_lengths.shape, jnp.int32),
                pltpu.SMEM(range_shift.shape, jnp.int32),
                pltpu.VMEM((slots, width), hidden.dtype),
                pltpu.VMEM((n_dp * PARTS, depth // PARTS, columns), qkv_weight.dtype),
                pltpu.VMEM((slots, columns), jnp.float32),
                pltpu.VMEM((n_sp, 8, 128), jnp.int32),
                pltpu.VMEM((rows_dev, columns), hidden.dtype),
                pltpu.VMEM((edge, columns), hidden.dtype),
                dma((5 + PARTS,)),
                dma(((n_dp + 2) * PARTS,)),
                dma((n_dp * PARTS,)),
                dma((others, 2)),
                dma((others, 2)),
                dma((others, 2)),
                dma((others, 2)),
                dma((others, shares)),
                dma((others, shares)),
                dma((n_sp - 1,)),
                dma((n_sp - 1,)),
                dma((2,)),
                dma((2,)),
            ],
            compiler_params=pltpu.CompilerParams(
                collective_id=0, has_side_effects=True, vmem_limit_bytes=63 * 1024 * 1024
            ),
            cost_estimate=pl.CostEstimate(
                flops=2 * slots * width * columns,
                bytes_accessed=2 * width * (rows_dev + columns),
                transcendentals=rows_dev * rows_dev,
            ),
        )(hidden, pad_counts, doc_lengths, range_shift, qkv_weight)

    in_specs = (P("dp", "sp", None), P("dp", "sp"), P("dp", None), P("dp", None), P("dp", None))
    return jax.shard_map(
        step, mesh=mesh, in_specs=in_specs, out_specs=P("dp", "sp", None), check_vma=False
    )
```

```python
import functools
import math

import jax
import jax.numpy as jnp
from jax import lax
from jax.experimental import pallas as pl
from jax.experimental.pallas import tpu as pltpu
from jax.sharding import PartitionSpec as P

MESH = pl.DeviceIdType.MESH
PARTS = 2


def flipped(index, bits):
    out, bit = index, 1
    while bit <= bits:
        if bits & bit:
            out = out + bit - 2 * bit * ((index // bit) % 2)
        bit *= 2
    return out


def flipped(index, bits):
    out, bit = index, 1
    while bit <= bits:
        if bits & bit:
            out = out + bit - 2 * bit * ((index // bit) % 2)
        bit *= 2
    return out


def nearest_first(index, count):
    both = jnp.minimum(index, count - 1 - index)
    longer = jnp.where(index <= count - 1 - index, 1, -1)
    out = []
    for j in range(1, count):
        near = (j + 1) // 2 if j % 2 else -(j // 2)
        out.append(index + jnp.where(j <= 2 * both, near, longer * (j - both)))
    return out


def travel_order(index, count, parts):
    near = nearest_first(index, count)
    both = jnp.minimum(index, count - 1 - index)
    out = []
    for pair in range(0, count - 1, 2):
        if pair + 1 == count - 1:
            out += [(near[pair], part) for part in range(parts)]
            continue
        two_sided = pair // 2 < both
        for step in range(2 * parts):
            shard = jnp.where(two_sided, near[pair + step % 2], near[pair + step // parts])
            out.append((shard, jnp.where(two_sided, step // 2, step % parts)))
    return out


def share_count(chips, depth):
    for shares in (4, 2):
        halves = 2 if shares == 4 else 1
        if chips % shares == 0 and depth % (2 * shares * halves * 16) == 0:
            return shares
    return 1


def kernel(
    n_sp,
    n_dp,
    shares,
    hidden_ref,
    pad_hbm,
    docs_hbm,
    shift_hbm,
    weight_ref,
    out_ref,
    pad_ref,
    docs_ref,
    shift_ref,
    rows_buf,
    weights,
    total,
    pads,
    cand,
    head,
    local_sem,
    z_send,
    z_recv,
    plane_send,
    plane_recv,
    diag_send,
    diag_recv,
    sib_send,
    sib_recv,
    pad_send,
    pad_recv,
    edge_send,
    edge_recv,
):
    sp, dp = lax.axis_index("sp"), lax.axis_index("dp")
    rows_dev = hidden_ref.shape[1]
    depth, columns = weight_ref.shape
    head_dim = columns // 3
    least_pad = rows_dev // 4
    slots = rows_dev - least_pad
    edge = rows_dev // 8
    core = sp % 2
    place = (sp // 2) % shares
    sibling = flipped(sp, 1)
    part_depth = depth // PARTS
    piece = part_depth // (2 * shares)
    over_x, over_y, over_xy = flipped(place, 1), flipped(place, 2), flipped(place, 3)
    x_peer, y_peer = flipped(sp, 2), flipped(sp, 4)
    units = travel_order(dp, n_dp, PARTS)
    origins = [shard for shard, _ in units]
    shards = [shard * PARTS + part for shard, part in units]
    n_units = len(units)
    inner = (dp > 0) & (dp < n_dp - 1)
    prior, later = (sp + n_sp - 1) % n_sp, (sp + 1) % n_sp

    def rows_of(which_core, which_place, half=None):
        start = (which_core * shares + which_place) * piece
        if half is None:
            return pl.ds(pl.multiple_of(start, 16), piece)
        return pl.ds(pl.multiple_of(start + half * (piece // 2), 16), piece // 2)

    def half_of(which_core):
        half = part_depth // 2
        return pl.ds(pl.multiple_of(which_core * half, 16), half)

    fetch_rows = pltpu.make_async_copy(
        hidden_ref.at[0, pl.ds(least_pad, slots), :], rows_buf, local_sem.at[0]
    )
    fetch_rows.start()
    fetch_weights = [
        pltpu.make_async_copy(
            weight_ref.at[pl.ds(part * part_depth, part_depth), :],
            weights.at[dp * PARTS + part],
            local_sem.at[5 + part],
        )
        for part in range(PARTS)
    ]
    for fetch in fetch_weights:
        fetch.start()
    fetch_pad = pltpu.make_async_copy(pad_hbm, pad_ref, local_sem.at[2])
    fetch_pad.start()
    fetch_docs = pltpu.make_async_copy(docs_hbm, docs_ref, local_sem.at[3])
    fetch_docs.start()
    fetch_shift = pltpu.make_async_copy(shift_hbm, shift_ref, local_sem.at[4])
    fetch_shift.start()

    barrier = pltpu.get_barrier_semaphore()
    for j in range(1, n_sp):
        pl.semaphore_signal(
            barrier, inc=1, device_id={"sp": (sp + j) % n_sp}, device_id_type=MESH
        )
    for j in range(1, n_dp):
        pl.semaphore_signal(
            barrier, inc=1, device_id={"dp": (dp + j) % n_dp}, device_id_type=MESH
        )
    pl.semaphore_wait(barrier, n_sp - 1 + n_dp - 1)

    started = []

    def send(src, dst, send_sem, recv_sem, device, when=None):
        def copy():
            return pltpu.make_async_remote_copy(
                src_ref=src(),
                dst_ref=dst(),
                send_sem=send_sem,
                recv_sem=recv_sem,
                device_id=device,
                device_id_type=MESH,
            )

        if when is None:
            copy().start()
        else:
            pl.when(when)(lambda: copy().start())
        started.append((copy, when))

    def arrived(dst, send_sem, recv_sem, device):
        pltpu.make_async_remote_copy(
            src_ref=dst,
            dst_ref=dst,
            send_sem=send_sem,
            recv_sem=recv_sem,
            device_id=device,
            device_id_type=MESH,
        ).wait_recv()

    own = rows_of(core, place)
    for part in range(PARTS if n_dp > 1 else 0):
        mine = dp * PARTS + part
        start = part * part_depth + (core * shares + place) * piece
        own_source = lambda start=start: weight_ref.at[pl.ds(pl.multiple_of(start, 16), piece), :]
        own_target = lambda mine=mine: weights.at[mine, own, :]
        at = n_dp * PARTS + 2 * part
        send(own_source, own_target, z_send.at[at], z_recv.at[mine], {"dp": dp + 1}, dp < n_dp - 1)
        send(own_source, own_target, z_send.at[at + 1], z_recv.at[mine], {"dp": dp - 1}, dp > 0)
    fetch_pad.wait()
    padding = pad_ref[0, 0]
    pads[sp] = jnp.full(pads.shape[1:], padding, jnp.int32)
    for j in range(1, n_sp):
        block = lambda: pads.at[sp]
        send(block, block, pad_send.at[j - 1], pad_recv.at[j - 1], {"sp": (sp + j) % n_sp})

    def to_sibling(j, slot, rows):
        block = lambda: weights.at[shards[j], rows, :]
        send(block, block, sib_send.at[j, slot], sib_recv.at[j, slot], {"sp": sibling})

    def piece_copies(j):
        shard = shards[j]
        onward = jnp.where(origins[j] < dp, dp + 1, dp - 1)
        block = weights.at[shard, own, :]
        ways = [
            (z_send.at[shard], z_recv.at[shard], {"dp": onward}, (onward >= 0) & (onward < n_dp))
        ]
        if shares >= 2:
            ways.append((plane_send.at[j, 0], plane_recv.at[j, 0], {"sp": x_peer}, None))
        if shares >= 4:
            ways.append((plane_send.at[j, 1], plane_recv.at[j, 1], {"sp": y_peer}, None))
        if j == n_units - 1:
            ways.append((sib_send.at[j, 0], sib_recv.at[j, 0], {"sp": sibling}, None))
        return [
            (
                lambda ways=(out, into, peer): pltpu.make_async_remote_copy(
                    src_ref=block,
                    dst_ref=block,
                    send_sem=ways[0],
                    recv_sem=ways[1],
                    device_id=ways[2],
                    device_id_type=MESH,
                ),
                when,
            )
            for out, into, peer, when in ways
        ]

    def from_plane(j):
        shard = shards[j]
        origin = jnp.where(origins[j] < dp, dp - 1, dp + 1)
        arrived(weights.at[shard, own, :], z_send.at[shard], z_recv.at[shard], {"dp": origin})
        for copy, when in piece_copies(j):
            if when is None:
                copy().start()
            else:
                pl.when(when)(lambda: copy().start())

    def from_neighbours(j):
        if shares >= 2:
            rows = rows_of(core, over_x)
            arrived(weights.at[shards[j], rows, :], plane_send.at[j, 0], plane_recv.at[j, 0], {"sp": x_peer})
            if shares >= 4:
                block = lambda: weights.at[shards[j], rows_of(core, over_x, 0), :]
                send(block, block, diag_send.at[j, 0], diag_recv.at[j, 0], {"sp": y_peer})
            if j == n_units - 1:
                to_sibling(j, 1, rows)
        if shares >= 4:
            rows = rows_of(core, over_y)
            arrived(weights.at[shards[j], rows, :], plane_send.at[j, 1], plane_recv.at[j, 1], {"sp": y_peer})
            block = lambda: weights.at[shards[j], rows_of(core, over_y, 1), :]
            send(block, block, diag_send.at[j, 1], diag_recv.at[j, 1], {"sp": x_peer})
            if j == n_units - 1:
                to_sibling(j, 2, rows)

    def from_diagonal(j):
        if shares >= 4:
            for half, peer in ((0, y_peer), (1, x_peer)):
                block = weights.at[shards[j], rows_of(core, over_xy, half), :]
                arrived(block, diag_send.at[j, half], diag_recv.at[j, half], {"sp": peer})
        if j < n_units - 1:
            to_sibling(j, 0, half_of(core))
        elif shares >= 4:
            to_sibling(j, 3, rows_of(core, over_xy))

    def from_sibling(j):
        blocks = [half_of(1 - core)]
        if j == n_units - 1:
            blocks = [rows_of(1 - core, which) for which in (place, over_x, over_y, over_xy)[:shares]]
        for slot, rows in enumerate(blocks):
            block = weights.at[shards[j], rows, :]
            arrived(block, sib_send.at[j, slot], sib_recv.at[j, slot], {"sp": sibling})

    def product(unit):
        part = pl.ds(pl.multiple_of(unit * part_depth, 128), part_depth)
        return jnp.dot(rows_buf[:, part], weights[unit], preferred_element_type=jnp.float32)

    fetch_rows.wait()
    for fetch in fetch_weights:
        fetch.wait()
    total[...] = product(dp * PARTS)
    for part in range(1, PARTS):
        total[...] += product(dp * PARTS + part)
    for i in range(4):
        if i < n_units:
            if i < 2:
                from_plane(i)
            else:
                pl.when(inner)(functools.partial(from_plane, i))
    for i in range(n_units):
        from_neighbours(i)
        if i + 4 < n_units:
            pl.when(inner)(functools.partial(from_plane, i + 4))
        if i + 2 < n_units:
            pl.when(~inner)(functools.partial(from_plane, i + 2))
        if i >= 1:
            from_diagonal(i - 1)
        if i >= 2:
            from_sibling(i - 2)
            total[...] += product(shards[i - 2])

    for j in range(1, n_sp):
        block = pads.at[(sp + n_sp - j) % n_sp]
        arrived(block, pad_send.at[j - 1], pad_recv.at[j - 1], {"sp": (sp + j) % n_sp})
    before = jnp.zeros(pads.shape[1:], jnp.int32)
    for i in range(n_sp):
        before = before + jnp.where(i < sp, rows_dev - pads[i], 0)
    live = rows_dev - padding
    fetch_docs.wait()
    fetch_shift.wait()
    shift = jnp.where(sp == 0, 0, shift_ref[0, sp])
    next_shift = jnp.where(sp == n_sp - 1, 0, shift_ref[0, later])
    owned_count = live + next_shift - shift
    docs = docs_ref.shape[1]
    lengths = jnp.broadcast_to(docs_ref[...].astype(jnp.float32), (8, docs)).astype(jnp.bfloat16)
    upper = (
        lax.broadcasted_iota(jnp.int32, (docs, docs), 0)
        <= lax.broadcasted_iota(jnp.int32, (docs, docs), 1)
    ).astype(jnp.float32).astype(jnp.bfloat16)
    ends = jnp.dot(lengths, upper, preferred_element_type=jnp.float32)[0:1].astype(jnp.int32)
    row = lax.broadcasted_iota(jnp.int32, (rows_dev, rows_dev), 0)
    col = lax.broadcasted_iota(jnp.int32, (rows_dev, rows_dev), 1)
    doc_row = lax.broadcasted_iota(jnp.int32, (rows_dev, docs), 0)
    local_ends = jnp.broadcast_to(ends - before[0:1, 0:1] - shift, (rows_dev, docs))
    doc_start = jnp.max(
        jnp.where(local_ends <= doc_row, local_ends, -(before[0:1, 0:1] + shift)).astype(jnp.float32),
        axis=1,
        keepdims=True,
    )
    allowed = (col <= row) & (col.astype(jnp.float32) >= doc_start)
    moved = row + shift
    target = jnp.where(
        moved < 0, edge + moved, jnp.where(moved < live, padding + moved, edge + moved - live)
    )
    pick = ((col == target) & (row < owned_count)).astype(jnp.float32).astype(jnp.bfloat16)
    head_row = lax.broadcasted_iota(jnp.int32, (edge, slots), 0)
    head_col = lax.broadcasted_iota(jnp.int32, (edge, slots), 1)
    head_pick = (head_col == head_row + padding - least_pad).astype(jnp.float32).astype(jnp.bfloat16)
    query_live = lax.broadcasted_iota(jnp.int32, (rows_dev, head_dim), 0) < owned_count

    if n_units:
        from_diagonal(n_units - 1)
        from_sibling(n_units - 2)
        total[...] += product(shards[n_units - 2])
        from_sibling(n_units - 1)
        total[...] += product(shards[n_units - 1])
    projected = total[...].astype(jnp.bfloat16)

    own_rows = pl.ds(2 * edge, slots)
    cand[own_rows, :] = projected
    tail = cand.at[pl.ds(rows_dev - edge, edge), :]
    send(lambda: tail, lambda: cand.at[pl.ds(0, edge), :], edge_send.at[0], edge_recv.at[0], {"sp": later})
    head[...] = jnp.dot(head_pick, projected, preferred_element_type=jnp.float32).astype(jnp.bfloat16)
    send(lambda: head, lambda: cand.at[pl.ds(edge, edge), :], edge_send.at[1], edge_recv.at[1], {"sp": prior})
    sent_edges = [copy for copy, _ in started[-2:]]
    del started[-2:]
    for j in range(n_units):
        started.extend(piece_copies(j))
    for copy, when in started:
        if when is None:
            copy().wait_send()
        else:
            pl.when(when)(lambda: copy().wait_send())
    arrived(cand.at[pl.ds(0, edge), :], edge_send.at[0], edge_recv.at[0], {"sp": later})
    arrived(cand.at[pl.ds(edge, edge), :], edge_send.at[1], edge_recv.at[1], {"sp": prior})

    qkv = jnp.dot(pick, cand[...], preferred_element_type=jnp.float32).astype(jnp.bfloat16)
    query, keys, values = qkv[:, :head_dim], qkv[:, head_dim : 2 * head_dim], qkv[:, 2 * head_dim :]
    scores = lax.dot_general(
        query, keys, (((1,), (1,)), ((), ())), preferred_element_type=jnp.float32
    ) * (1.0 / math.sqrt(head_dim))
    masked = jnp.where(allowed, scores, -1e30)
    peak = jnp.max(masked, axis=1, keepdims=True)
    exponent = jnp.where(allowed, jnp.exp(masked - peak), 0.0)
    probs = (exponent / jnp.sum(exponent, axis=1, keepdims=True)).astype(jnp.bfloat16)
    result = jnp.dot(probs, values, preferred_element_type=jnp.float32)
    out_ref[0] = jnp.where(query_live, result, 0.0).astype(out_ref.dtype)
    sent_edges[0]().wait_send()
    sent_edges[1]().wait_send()


def solution(mesh):
    n_sp, n_dp = mesh.shape["sp"], mesh.shape["dp"]

    def step(hidden, pad_counts, doc_lengths, range_shift, qkv_weight):
        rows_dev, width = hidden.shape[1:]
        depth, columns = qkv_weight.shape
        shares = share_count(n_sp // 2, depth // PARTS)
        edge, slots = rows_dev // 8, rows_dev - rows_dev // 4
        others = max(n_dp - 1, 1) * PARTS
        dma = pltpu.SemaphoreType.DMA
        return pl.pallas_call(
            functools.partial(kernel, n_sp, n_dp, shares),
            out_shape=jax.ShapeDtypeStruct((1, rows_dev, columns // 3), hidden.dtype),
            in_specs=[
                pl.BlockSpec(memory_space=pltpu.HBM),
            ]
            * 5,
            out_specs=pl.BlockSpec(memory_space=pltpu.VMEM),
            scratch_shapes=[
                pltpu.SMEM(pad_counts.shape, jnp.int32),
                pltpu.VMEM(doc_lengths.shape, jnp.int32),
                pltpu.SMEM(range_shift.shape, jnp.int32),
                pltpu.VMEM((slots, width), hidden.dtype),
                pltpu.VMEM((n_dp * PARTS, depth // PARTS, columns), qkv_weight.dtype),
                pltpu.VMEM((slots, columns), jnp.float32),
                pltpu.VMEM((n_sp, 8, 128), jnp.int32),
                pltpu.VMEM((rows_dev, columns), hidden.dtype),
                pltpu.VMEM((edge, columns), hidden.dtype),
                dma((5 + PARTS,)),
                dma(((n_dp + 2) * PARTS,)),
                dma((n_dp * PARTS,)),
                dma((others, 2)),
                dma((others, 2)),
                dma((others, 2)),
                dma((others, 2)),
                dma((others, shares)),
                dma((others, shares)),
                dma((n_sp - 1,)),
                dma((n_sp - 1,)),
                dma((2,)),
                dma((2,)),
            ],
            compiler_params=pltpu.CompilerParams(
                collective_id=0, has_side_effects=True, vmem_limit_bytes=63 * 1024 * 1024
            ),
            cost_estimate=pl.CostEstimate(
                flops=2 * slots * width * columns,
                bytes_accessed=2 * width * (rows_dev + columns),
                transcendentals=rows_dev * rows_dev,
            ),
        )(hidden, pad_counts, doc_lengths, range_shift, qkv_weight)

    in_specs = (P("dp", "sp", None), P("dp", "sp"), P("dp", None), P("dp", None), P("dp", None))
    return jax.shard_map(
        step, mesh=mesh, in_specs=in_specs, out_specs=P("dp", "sp", None), check_vma=False
    )
```

```python
import functools
import math

import jax
import jax.numpy as jnp
from jax import lax
from jax.experimental import pallas as pl
from jax.experimental.pallas import tpu as pltpu
from jax.sharding import PartitionSpec as P

MESH = pl.DeviceIdType.MESH
PARTS = 4


def flipped(index, bits):
    out, bit = index, 1
    while bit <= bits:
        if bits & bit:
            out = out + bit - 2 * bit * ((index // bit) % 2)
        bit *= 2
    return out


def flipped(index, bits):
    out, bit = index, 1
    while bit <= bits:
        if bits & bit:
            out = out + bit - 2 * bit * ((index // bit) % 2)
        bit *= 2
    return out


def nearest_first(index, count):
    both = jnp.minimum(index, count - 1 - index)
    longer = jnp.where(index <= count - 1 - index, 1, -1)
    out = []
    for j in range(1, count):
        near = (j + 1) // 2 if j % 2 else -(j // 2)
        out.append(index + jnp.where(j <= 2 * both, near, longer * (j - both)))
    return out


def travel_order(index, count, parts):
    near = nearest_first(index, count)
    both = jnp.minimum(index, count - 1 - index)
    out = []
    for pair in range(0, count - 1, 2):
        if pair + 1 == count - 1:
            out += [(near[pair], part) for part in range(parts)]
            continue
        two_sided = pair // 2 < both
        for step in range(2 * parts):
            shard = jnp.where(two_sided, near[pair + step % 2], near[pair + step // parts])
            out.append((shard, jnp.where(two_sided, step // 2, step % parts)))
    return out


def share_count(chips, depth):
    for shares in (4, 2):
        halves = 2 if shares == 4 else 1
        if chips % shares == 0 and depth % (2 * shares * halves * 16) == 0:
            return shares
    return 1


def kernel(
    n_sp,
    n_dp,
    shares,
    hidden_ref,
    pad_hbm,
    docs_hbm,
    shift_hbm,
    weight_ref,
    out_ref,
    pad_ref,
    docs_ref,
    shift_ref,
    rows_buf,
    weights,
    total,
    pads,
    cand,
    head,
    local_sem,
    z_send,
    z_recv,
    plane_send,
    plane_recv,
    diag_send,
    diag_recv,
    sib_send,
    sib_recv,
    pad_send,
    pad_recv,
    edge_send,
    edge_recv,
):
    sp, dp = lax.axis_index("sp"), lax.axis_index("dp")
    rows_dev = hidden_ref.shape[1]
    depth, columns = weight_ref.shape
    head_dim = columns // 3
    least_pad = rows_dev // 4
    slots = rows_dev - least_pad
    edge = rows_dev // 8
    core = sp % 2
    place = (sp // 2) % shares
    sibling = flipped(sp, 1)
    part_depth = depth // PARTS
    piece = part_depth // (2 * shares)
    over_x, over_y, over_xy = flipped(place, 1), flipped(place, 2), flipped(place, 3)
    x_peer, y_peer = flipped(sp, 2), flipped(sp, 4)
    units = travel_order(dp, n_dp, PARTS)
    origins = [shard for shard, _ in units]
    shards = [shard * PARTS + part for shard, part in units]
    n_units = len(units)
    inner = (dp > 0) & (dp < n_dp - 1)
    prior, later = (sp + n_sp - 1) % n_sp, (sp + 1) % n_sp

    def rows_of(which_core, which_place, half=None):
        start = (which_core * shares + which_place) * piece
        if half is None:
            return pl.ds(pl.multiple_of(start, 16), piece)
        return pl.ds(pl.multiple_of(start + half * (piece // 2), 16), piece // 2)

    def half_of(which_core):
        half = part_depth // 2
        return pl.ds(pl.multiple_of(which_core * half, 16), half)

    fetch_rows = pltpu.make_async_copy(
        hidden_ref.at[0, pl.ds(least_pad, slots), :], rows_buf, local_sem.at[0]
    )
    fetch_rows.start()
    fetch_weights = [
        pltpu.make_async_copy(
            weight_ref.at[pl.ds(part * part_depth, part_depth), :],
            weights.at[dp * PARTS + part],
            local_sem.at[5 + part],
        )
        for part in range(PARTS)
    ]
    for fetch in fetch_weights:
        fetch.start()
    fetch_pad = pltpu.make_async_copy(pad_hbm, pad_ref, local_sem.at[2])
    fetch_pad.start()
    fetch_docs = pltpu.make_async_copy(docs_hbm, docs_ref, local_sem.at[3])
    fetch_docs.start()
    fetch_shift = pltpu.make_async_copy(shift_hbm, shift_ref, local_sem.at[4])
    fetch_shift.start()

    barrier = pltpu.get_barrier_semaphore()
    for j in range(1, n_sp):
        pl.semaphore_signal(
            barrier, inc=1, device_id={"sp": (sp + j) % n_sp}, device_id_type=MESH
        )
    for j in range(1, n_dp):
        pl.semaphore_signal(
            barrier, inc=1, device_id={"dp": (dp + j) % n_dp}, device_id_type=MESH
        )
    pl.semaphore_wait(barrier, n_sp - 1 + n_dp - 1)

    started = []

    def send(src, dst, send_sem, recv_sem, device, when=None):
        def copy():
            return pltpu.make_async_remote_copy(
                src_ref=src(),
                dst_ref=dst(),
                send_sem=send_sem,
                recv_sem=recv_sem,
                device_id=device,
                device_id_type=MESH,
            )

        if when is None:
            copy().start()
        else:
            pl.when(when)(lambda: copy().start())
        started.append((copy, when))

    def arrived(dst, send_sem, recv_sem, device):
        pltpu.make_async_remote_copy(
            src_ref=dst,
            dst_ref=dst,
            send_sem=send_sem,
            recv_sem=recv_sem,
            device_id=device,
            device_id_type=MESH,
        ).wait_recv()

    own = rows_of(core, place)
    for part in range(PARTS if n_dp > 1 else 0):
        mine = dp * PARTS + part
        start = part * part_depth + (core * shares + place) * piece
        own_source = lambda start=start: weight_ref.at[pl.ds(pl.multiple_of(start, 16), piece), :]
        own_target = lambda mine=mine: weights.at[mine, own, :]
        at = n_dp * PARTS + 2 * part
        send(own_source, own_target, z_send.at[at], z_recv.at[mine], {"dp": dp + 1}, dp < n_dp - 1)
        send(own_source, own_target, z_send.at[at + 1], z_recv.at[mine], {"dp": dp - 1}, dp > 0)
    fetch_pad.wait()
    padding = pad_ref[0, 0]
    pads[sp] = jnp.full(pads.shape[1:], padding, jnp.int32)
    for j in range(1, n_sp):
        block = lambda: pads.at[sp]
        send(block, block, pad_send.at[j - 1], pad_recv.at[j - 1], {"sp": (sp + j) % n_sp})

    def to_sibling(j, slot, rows):
        block = lambda: weights.at[shards[j], rows, :]
        send(block, block, sib_send.at[j, slot], sib_recv.at[j, slot], {"sp": sibling})

    def piece_copies(j):
        shard = shards[j]
        onward = jnp.where(origins[j] < dp, dp + 1, dp - 1)
        block = weights.at[shard, own, :]
        ways = [
            (z_send.at[shard], z_recv.at[shard], {"dp": onward}, (onward >= 0) & (onward < n_dp))
        ]
        if shares >= 2:
            ways.append((plane_send.at[j, 0], plane_recv.at[j, 0], {"sp": x_peer}, None))
        if shares >= 4:
            ways.append((plane_send.at[j, 1], plane_recv.at[j, 1], {"sp": y_peer}, None))
        if j == n_units - 1:
            ways.append((sib_send.at[j, 0], sib_recv.at[j, 0], {"sp": sibling}, None))
        return [
            (
                lambda ways=(out, into, peer): pltpu.make_async_remote_copy(
                    src_ref=block,
                    dst_ref=block,
                    send_sem=ways[0],
                    recv_sem=ways[1],
                    device_id=ways[2],
                    device_id_type=MESH,
                ),
                when,
            )
            for out, into, peer, when in ways
        ]

    def from_plane(j):
        shard = shards[j]
        origin = jnp.where(origins[j] < dp, dp - 1, dp + 1)
        arrived(weights.at[shard, own, :], z_send.at[shard], z_recv.at[shard], {"dp": origin})
        for copy, when in piece_copies(j):
            if when is None:
                copy().start()
            else:
                pl.when(when)(lambda: copy().start())

    def from_neighbours(j):
        if shares >= 2:
            rows = rows_of(core, over_x)
            arrived(weights.at[shards[j], rows, :], plane_send.at[j, 0], plane_recv.at[j, 0], {"sp": x_peer})
            if shares >= 4:
                block = lambda: weights.at[shards[j], rows_of(core, over_x, 0), :]
                send(block, block, diag_send.at[j, 0], diag_recv.at[j, 0], {"sp": y_peer})
            if j == n_units - 1:
                to_sibling(j, 1, rows)
        if shares >= 4:
            rows = rows_of(core, over_y)
            arrived(weights.at[shards[j], rows, :], plane_send.at[j, 1], plane_recv.at[j, 1], {"sp": y_peer})
            block = lambda: weights.at[shards[j], rows_of(core, over_y, 1), :]
            send(block, block, diag_send.at[j, 1], diag_recv.at[j, 1], {"sp": x_peer})
            if j == n_units - 1:
                to_sibling(j, 2, rows)

    def from_diagonal(j):
        if shares >= 4:
            for half, peer in ((0, y_peer), (1, x_peer)):
                block = weights.at[shards[j], rows_of(core, over_xy, half), :]
                arrived(block, diag_send.at[j, half], diag_recv.at[j, half], {"sp": peer})
        if j < n_units - 1:
            to_sibling(j, 0, half_of(core))
        elif shares >= 4:
            to_sibling(j, 3, rows_of(core, over_xy))

    def from_sibling(j):
        blocks = [half_of(1 - core)]
        if j == n_units - 1:
            blocks = [rows_of(1 - core, which) for which in (place, over_x, over_y, over_xy)[:shares]]
        for slot, rows in enumerate(blocks):
            block = weights.at[shards[j], rows, :]
            arrived(block, sib_send.at[j, slot], sib_recv.at[j, slot], {"sp": sibling})

    def product(unit):
        part = pl.ds(pl.multiple_of(unit * part_depth, 128), part_depth)
        return jnp.dot(rows_buf[:, part], weights[unit], preferred_element_type=jnp.float32)

    fetch_rows.wait()
    for fetch in fetch_weights:
        fetch.wait()
    total[...] = product(dp * PARTS)
    for part in range(1, PARTS):
        total[...] += product(dp * PARTS + part)
    for i in range(2 * PARTS):
        if i < n_units:
            if i < PARTS:
                from_plane(i)
            else:
                pl.when(inner)(functools.partial(from_plane, i))
    for i in range(n_units):
        from_neighbours(i)
        if i + 2 * PARTS < n_units:
            pl.when(inner)(functools.partial(from_plane, i + 2 * PARTS))
        if i + PARTS < n_units:
            pl.when(~inner)(functools.partial(from_plane, i + PARTS))
        if i >= 1:
            from_diagonal(i - 1)
        if i >= 2:
            from_sibling(i - 2)
            total[...] += product(shards[i - 2])

    for j in range(1, n_sp):
        block = pads.at[(sp + n_sp - j) % n_sp]
        arrived(block, pad_send.at[j - 1], pad_recv.at[j - 1], {"sp": (sp + j) % n_sp})
    before = jnp.zeros(pads.shape[1:], jnp.int32)
    for i in range(n_sp):
        before = before + jnp.where(i < sp, rows_dev - pads[i], 0)
    live = rows_dev - padding
    fetch_docs.wait()
    fetch_shift.wait()
    shift = jnp.where(sp == 0, 0, shift_ref[0, sp])
    next_shift = jnp.where(sp == n_sp - 1, 0, shift_ref[0, later])
    owned_count = live + next_shift - shift
    docs = docs_ref.shape[1]
    lengths = jnp.broadcast_to(docs_ref[...].astype(jnp.float32), (8, docs)).astype(jnp.bfloat16)
    upper = (
        lax.broadcasted_iota(jnp.int32, (docs, docs), 0)
        <= lax.broadcasted_iota(jnp.int32, (docs, docs), 1)
    ).astype(jnp.float32).astype(jnp.bfloat16)
    ends = jnp.dot(lengths, upper, preferred_element_type=jnp.float32)[0:1].astype(jnp.int32)
    row = lax.broadcasted_iota(jnp.int32, (rows_dev, rows_dev), 0)
    col = lax.broadcasted_iota(jnp.int32, (rows_dev, rows_dev), 1)
    doc_row = lax.broadcasted_iota(jnp.int32, (rows_dev, docs), 0)
    local_ends = jnp.broadcast_to(ends - before[0:1, 0:1] - shift, (rows_dev, docs))
    doc_start = jnp.max(
        jnp.where(local_ends <= doc_row, local_ends, -(before[0:1, 0:1] + shift)).astype(jnp.float32),
        axis=1,
        keepdims=True,
    )
    allowed = (col <= row) & (col.astype(jnp.float32) >= doc_start)
    moved = row + shift
    target = jnp.where(
        moved < 0, edge + moved, jnp.where(moved < live, padding + moved, edge + moved - live)
    )
    pick = ((col == target) & (row < owned_count)).astype(jnp.float32).astype(jnp.bfloat16)
    head_row = lax.broadcasted_iota(jnp.int32, (edge, slots), 0)
    head_col = lax.broadcasted_iota(jnp.int32, (edge, slots), 1)
    head_pick = (head_col == head_row + padding - least_pad).astype(jnp.float32).astype(jnp.bfloat16)
    query_live = lax.broadcasted_iota(jnp.int32, (rows_dev, head_dim), 0) < owned_count

    if n_units:
        from_diagonal(n_units - 1)
        from_sibling(n_units - 2)
        total[...] += product(shards[n_units - 2])
        from_sibling(n_units - 1)
        total[...] += product(shards[n_units - 1])
    projected = total[...].astype(jnp.bfloat16)

    own_rows = pl.ds(2 * edge, slots)
    cand[own_rows, :] = projected
    tail = cand.at[pl.ds(rows_dev - edge, edge), :]
    send(lambda: tail, lambda: cand.at[pl.ds(0, edge), :], edge_send.at[0], edge_recv.at[0], {"sp": later})
    head[...] = jnp.dot(head_pick, projected, preferred_element_type=jnp.float32).astype(jnp.bfloat16)
    send(lambda: head, lambda: cand.at[pl.ds(edge, edge), :], edge_send.at[1], edge_recv.at[1], {"sp": prior})
    sent_edges = [copy for copy, _ in started[-2:]]
    del started[-2:]
    for j in range(n_units):
        started.extend(piece_copies(j))
    for copy, when in started:
        if when is None:
            copy().wait_send()
        else:
            pl.when(when)(lambda: copy().wait_send())
    arrived(cand.at[pl.ds(0, edge), :], edge_send.at[0], edge_recv.at[0], {"sp": later})
    arrived(cand.at[pl.ds(edge, edge), :], edge_send.at[1], edge_recv.at[1], {"sp": prior})

    qkv = jnp.dot(pick, cand[...], preferred_element_type=jnp.float32).astype(jnp.bfloat16)
    query, keys, values = qkv[:, :head_dim], qkv[:, head_dim : 2 * head_dim], qkv[:, 2 * head_dim :]
    scores = lax.dot_general(
        query, keys, (((1,), (1,)), ((), ())), preferred_element_type=jnp.float32
    ) * (1.0 / math.sqrt(head_dim))
    masked = jnp.where(allowed, scores, -1e30)
    peak = jnp.max(masked, axis=1, keepdims=True)
    exponent = jnp.where(allowed, jnp.exp(masked - peak), 0.0)
    probs = (exponent / jnp.sum(exponent, axis=1, keepdims=True)).astype(jnp.bfloat16)
    result = jnp.dot(probs, values, preferred_element_type=jnp.float32)
    out_ref[0] = jnp.where(query_live, result, 0.0).astype(out_ref.dtype)
    sent_edges[0]().wait_send()
    sent_edges[1]().wait_send()


def solution(mesh):
    n_sp, n_dp = mesh.shape["sp"], mesh.shape["dp"]

    def step(hidden, pad_counts, doc_lengths, range_shift, qkv_weight):
        rows_dev, width = hidden.shape[1:]
        depth, columns = qkv_weight.shape
        shares = share_count(n_sp // 2, depth // PARTS)
        edge, slots = rows_dev // 8, rows_dev - rows_dev // 4
        others = max(n_dp - 1, 1) * PARTS
        dma = pltpu.SemaphoreType.DMA
        return pl.pallas_call(
            functools.partial(kernel, n_sp, n_dp, shares),
            out_shape=jax.ShapeDtypeStruct((1, rows_dev, columns // 3), hidden.dtype),
            in_specs=[
                pl.BlockSpec(memory_space=pltpu.HBM),
            ]
            * 5,
            out_specs=pl.BlockSpec(memory_space=pltpu.VMEM),
            scratch_shapes=[
                pltpu.SMEM(pad_counts.shape, jnp.int32),
                pltpu.VMEM(doc_lengths.shape, jnp.int32),
                pltpu.SMEM(range_shift.shape, jnp.int32),
                pltpu.VMEM((slots, width), hidden.dtype),
                pltpu.VMEM((n_dp * PARTS, depth // PARTS, columns), qkv_weight.dtype),
                pltpu.VMEM((slots, columns), jnp.float32),
                pltpu.VMEM((n_sp, 8, 128), jnp.int32),
                pltpu.VMEM((rows_dev, columns), hidden.dtype),
                pltpu.VMEM((edge, columns), hidden.dtype),
                dma((5 + PARTS,)),
                dma(((n_dp + 2) * PARTS,)),
                dma((n_dp * PARTS,)),
                dma((others, 2)),
                dma((others, 2)),
                dma((others, 2)),
                dma((others, 2)),
                dma((others, shares)),
                dma((others, shares)),
                dma((n_sp - 1,)),
                dma((n_sp - 1,)),
                dma((2,)),
                dma((2,)),
            ],
            compiler_params=pltpu.CompilerParams(
                collective_id=0, has_side_effects=True, vmem_limit_bytes=63 * 1024 * 1024
            ),
            cost_estimate=pl.CostEstimate(
                flops=2 * slots * width * columns,
                bytes_accessed=2 * width * (rows_dev + columns),
                transcendentals=rows_dev * rows_dev,
            ),
        )(hidden, pad_counts, doc_lengths, range_shift, qkv_weight)

    in_specs = (P("dp", "sp", None), P("dp", "sp"), P("dp", None), P("dp", None), P("dp", None))
    return jax.shard_map(
        step, mesh=mesh, in_specs=in_specs, out_specs=P("dp", "sp", None), check_vma=False
    )
```

```python
import functools
import math

import jax
import jax.numpy as jnp
from jax import lax
from jax.experimental import pallas as pl
from jax.experimental.pallas import tpu as pltpu
from jax.sharding import PartitionSpec as P

MESH = pl.DeviceIdType.MESH
PARTS = 2


def flipped(index, bits):
    out, bit = index, 1
    while bit <= bits:
        if bits & bit:
            out = out + bit - 2 * bit * ((index // bit) % 2)
        bit *= 2
    return out


def flipped(index, bits):
    out, bit = index, 1
    while bit <= bits:
        if bits & bit:
            out = out + bit - 2 * bit * ((index // bit) % 2)
        bit *= 2
    return out


def nearest_first(index, count):
    both = jnp.minimum(index, count - 1 - index)
    longer = jnp.where(index <= count - 1 - index, 1, -1)
    out = []
    for j in range(1, count):
        near = (j + 1) // 2 if j % 2 else -(j // 2)
        out.append(index + jnp.where(j <= 2 * both, near, longer * (j - both)))
    return out


def travel_order(index, count, parts):
    near = nearest_first(index, count)
    both = jnp.minimum(index, count - 1 - index)
    out = []
    for pair in range(0, count - 1, 2):
        if pair + 1 == count - 1:
            out += [(near[pair], part) for part in range(parts)]
            continue
        two_sided = pair // 2 < both
        for step in range(2 * parts):
            shard = jnp.where(two_sided, near[pair + step % 2], near[pair + step // parts])
            out.append((shard, jnp.where(two_sided, step // 2, step % parts)))
    return out


def share_count(chips, depth):
    for shares in (4, 2):
        halves = 2 if shares == 4 else 1
        if chips % shares == 0 and depth % (2 * shares * halves * 16) == 0:
            return shares
    return 1


def kernel(
    n_sp,
    n_dp,
    shares,
    hidden_ref,
    pad_hbm,
    docs_hbm,
    shift_hbm,
    weight_ref,
    out_ref,
    pad_ref,
    docs_ref,
    shift_ref,
    rows_buf,
    weights,
    total,
    pads,
    cand,
    head,
    local_sem,
    z_send,
    z_recv,
    plane_send,
    plane_recv,
    diag_send,
    diag_recv,
    sib_send,
    sib_recv,
    pad_send,
    pad_recv,
    edge_send,
    edge_recv,
):
    sp, dp = lax.axis_index("sp"), lax.axis_index("dp")
    rows_dev = hidden_ref.shape[1]
    depth, columns = weight_ref.shape
    head_dim = columns // 3
    least_pad = rows_dev // 4
    slots = rows_dev - least_pad
    edge = rows_dev // 8
    core = sp % 2
    place = (sp // 2) % shares
    sibling = flipped(sp, 1)
    part_depth = depth // PARTS
    piece = part_depth // (2 * shares)
    over_x, over_y, over_xy = flipped(place, 1), flipped(place, 2), flipped(place, 3)
    x_peer, y_peer = flipped(sp, 2), flipped(sp, 4)
    units = travel_order(dp, n_dp, PARTS)
    origins = [shard for shard, _ in units]
    shards = [shard * PARTS + part for shard, part in units]
    n_units = len(units)
    inner = (dp > 0) & (dp < n_dp - 1)
    prior, later = (sp + n_sp - 1) % n_sp, (sp + 1) % n_sp

    def rows_of(which_core, which_place, half=None):
        start = (which_core * shares + which_place) * piece
        if half is None:
            return pl.ds(pl.multiple_of(start, 16), piece)
        return pl.ds(pl.multiple_of(start + half * (piece // 2), 16), piece // 2)

    def half_of(which_core):
        half = part_depth // 2
        return pl.ds(pl.multiple_of(which_core * half, 16), half)

    fetch_rows = pltpu.make_async_copy(
        hidden_ref.at[0, pl.ds(least_pad, slots), :], rows_buf, local_sem.at[0]
    )
    fetch_rows.start()
    fetch_weights = [
        pltpu.make_async_copy(
            weight_ref.at[pl.ds(part * part_depth, part_depth), :],
            weights.at[dp * PARTS + part],
            local_sem.at[5 + part],
        )
        for part in range(PARTS)
    ]
    for fetch in fetch_weights:
        fetch.start()
    fetch_pad = pltpu.make_async_copy(pad_hbm, pad_ref, local_sem.at[2])
    fetch_pad.start()
    fetch_docs = pltpu.make_async_copy(docs_hbm, docs_ref, local_sem.at[3])
    fetch_docs.start()
    fetch_shift = pltpu.make_async_copy(shift_hbm, shift_ref, local_sem.at[4])
    fetch_shift.start()

    barrier = pltpu.get_barrier_semaphore()
    for j in range(1, n_sp):
        pl.semaphore_signal(
            barrier, inc=1, device_id={"sp": (sp + j) % n_sp}, device_id_type=MESH
        )
    for j in range(1, n_dp):
        pl.semaphore_signal(
            barrier, inc=1, device_id={"dp": (dp + j) % n_dp}, device_id_type=MESH
        )
    pl.semaphore_wait(barrier, n_sp - 1 + n_dp - 1)

    started = []

    def send(src, dst, send_sem, recv_sem, device, when=None):
        def copy():
            return pltpu.make_async_remote_copy(
                src_ref=src(),
                dst_ref=dst(),
                send_sem=send_sem,
                recv_sem=recv_sem,
                device_id=device,
                device_id_type=MESH,
            )

        if when is None:
            copy().start()
        else:
            pl.when(when)(lambda: copy().start())
        started.append((copy, when))

    def arrived(dst, send_sem, recv_sem, device):
        pltpu.make_async_remote_copy(
            src_ref=dst,
            dst_ref=dst,
            send_sem=send_sem,
            recv_sem=recv_sem,
            device_id=device,
            device_id_type=MESH,
        ).wait_recv()

    own = rows_of(core, place)
    for part in range(PARTS if n_dp > 1 else 0):
        mine = dp * PARTS + part
        start = part * part_depth + (core * shares + place) * piece
        own_source = lambda start=start: weight_ref.at[pl.ds(pl.multiple_of(start, 16), piece), :]
        own_target = lambda mine=mine: weights.at[mine, own, :]
        at = n_dp * PARTS + 2 * part
        send(own_source, own_target, z_send.at[at], z_recv.at[mine], {"dp": dp + 1}, dp < n_dp - 1)
        send(own_source, own_target, z_send.at[at + 1], z_recv.at[mine], {"dp": dp - 1}, dp > 0)
    fetch_pad.wait()
    padding = pad_ref[0, 0]
    pads[sp] = jnp.full(pads.shape[1:], padding, jnp.int32)
    for j in range(1, n_sp):
        block = lambda: pads.at[sp]
        send(block, block, pad_send.at[j - 1], pad_recv.at[j - 1], {"sp": (sp + j) % n_sp})

    def to_sibling(j, slot, rows):
        block = lambda: weights.at[shards[j], rows, :]
        send(block, block, sib_send.at[j, slot], sib_recv.at[j, slot], {"sp": sibling})

    def piece_copies(j):
        shard = shards[j]
        onward = jnp.where(origins[j] < dp, dp + 1, dp - 1)
        block = weights.at[shard, own, :]
        ways = [
            (z_send.at[shard], z_recv.at[shard], {"dp": onward}, (onward >= 0) & (onward < n_dp))
        ]
        if shares >= 2:
            ways.append((plane_send.at[j, 0], plane_recv.at[j, 0], {"sp": x_peer}, None))
        if shares >= 4:
            ways.append((plane_send.at[j, 1], plane_recv.at[j, 1], {"sp": y_peer}, None))
        if j == n_units - 1:
            ways.append((sib_send.at[j, 0], sib_recv.at[j, 0], {"sp": sibling}, None))
        return [
            (
                lambda ways=(out, into, peer): pltpu.make_async_remote_copy(
                    src_ref=block,
                    dst_ref=block,
                    send_sem=ways[0],
                    recv_sem=ways[1],
                    device_id=ways[2],
                    device_id_type=MESH,
                ),
                when,
            )
            for out, into, peer, when in ways
        ]

    def from_plane(j):
        shard = shards[j]
        origin = jnp.where(origins[j] < dp, dp - 1, dp + 1)
        arrived(weights.at[shard, own, :], z_send.at[shard], z_recv.at[shard], {"dp": origin})
        for copy, when in piece_copies(j):
            if when is None:
                copy().start()
            else:
                pl.when(when)(lambda: copy().start())

    def from_neighbours(j):
        if shares >= 2:
            rows = rows_of(core, over_x)
            arrived(weights.at[shards[j], rows, :], plane_send.at[j, 0], plane_recv.at[j, 0], {"sp": x_peer})
            if shares >= 4:
                block = lambda: weights.at[shards[j], rows_of(core, over_x, 0), :]
                send(block, block, diag_send.at[j, 0], diag_recv.at[j, 0], {"sp": y_peer})
            if j == n_units - 1:
                to_sibling(j, 1, rows)
        if shares >= 4:
            rows = rows_of(core, over_y)
            arrived(weights.at[shards[j], rows, :], plane_send.at[j, 1], plane_recv.at[j, 1], {"sp": y_peer})
            block = lambda: weights.at[shards[j], rows_of(core, over_y, 1), :]
            send(block, block, diag_send.at[j, 1], diag_recv.at[j, 1], {"sp": x_peer})
            if j == n_units - 1:
                to_sibling(j, 2, rows)

    def from_diagonal(j):
        if shares >= 4:
            for half, peer in ((0, y_peer), (1, x_peer)):
                block = weights.at[shards[j], rows_of(core, over_xy, half), :]
                arrived(block, diag_send.at[j, half], diag_recv.at[j, half], {"sp": peer})
        if j < n_units - 1:
            to_sibling(j, 0, half_of(core))
        elif shares >= 4:
            to_sibling(j, 3, rows_of(core, over_xy))

    def from_sibling(j):
        blocks = [half_of(1 - core)]
        if j == n_units - 1:
            blocks = [rows_of(1 - core, which) for which in (place, over_x, over_y, over_xy)[:shares]]
        for slot, rows in enumerate(blocks):
            block = weights.at[shards[j], rows, :]
            arrived(block, sib_send.at[j, slot], sib_recv.at[j, slot], {"sp": sibling})

    def product(unit):
        part = pl.ds(pl.multiple_of(unit * part_depth, 128), part_depth)
        return jnp.dot(rows_buf[:, part], weights[unit], preferred_element_type=jnp.float32)

    fetch_rows.wait()
    for fetch in fetch_weights:
        fetch.wait()
    total[...] = product(dp * PARTS)
    for part in range(1, PARTS):
        total[...] += product(dp * PARTS + part)
    for i in range(4):
        if i < n_units:
            if i < 2:
                from_plane(i)
            else:
                pl.when(inner)(functools.partial(from_plane, i))
    for i in range(n_units):
        from_neighbours(i)
        if i + 4 < n_units:
            pl.when(inner)(functools.partial(from_plane, i + 4))
        if i + 2 < n_units:
            pl.when(~inner)(functools.partial(from_plane, i + 2))
        if i >= 1:
            from_diagonal(i - 1)
        if i >= 2:
            from_sibling(i - 2)
            if i % 2:
                total[...] += product(shards[i - 3]) + product(shards[i - 2])

    for j in range(1, n_sp):
        block = pads.at[(sp + n_sp - j) % n_sp]
        arrived(block, pad_send.at[j - 1], pad_recv.at[j - 1], {"sp": (sp + j) % n_sp})
    before = jnp.zeros(pads.shape[1:], jnp.int32)
    for i in range(n_sp):
        before = before + jnp.where(i < sp, rows_dev - pads[i], 0)
    live = rows_dev - padding
    fetch_docs.wait()
    fetch_shift.wait()
    shift = jnp.where(sp == 0, 0, shift_ref[0, sp])
    next_shift = jnp.where(sp == n_sp - 1, 0, shift_ref[0, later])
    owned_count = live + next_shift - shift
    docs = docs_ref.shape[1]
    lengths = jnp.broadcast_to(docs_ref[...].astype(jnp.float32), (8, docs)).astype(jnp.bfloat16)
    upper = (
        lax.broadcasted_iota(jnp.int32, (docs, docs), 0)
        <= lax.broadcasted_iota(jnp.int32, (docs, docs), 1)
    ).astype(jnp.float32).astype(jnp.bfloat16)
    ends = jnp.dot(lengths, upper, preferred_element_type=jnp.float32)[0:1].astype(jnp.int32)
    row = lax.broadcasted_iota(jnp.int32, (rows_dev, rows_dev), 0)
    col = lax.broadcasted_iota(jnp.int32, (rows_dev, rows_dev), 1)
    doc_row = lax.broadcasted_iota(jnp.int32, (rows_dev, docs), 0)
    local_ends = jnp.broadcast_to(ends - before[0:1, 0:1] - shift, (rows_dev, docs))
    doc_start = jnp.max(
        jnp.where(local_ends <= doc_row, local_ends, -(before[0:1, 0:1] + shift)).astype(jnp.float32),
        axis=1,
        keepdims=True,
    )
    allowed = (col <= row) & (col.astype(jnp.float32) >= doc_start)
    moved = row + shift
    target = jnp.where(
        moved < 0, edge + moved, jnp.where(moved < live, padding + moved, edge + moved - live)
    )
    pick = ((col == target) & (row < owned_count)).astype(jnp.float32).astype(jnp.bfloat16)
    head_row = lax.broadcasted_iota(jnp.int32, (edge, slots), 0)
    head_col = lax.broadcasted_iota(jnp.int32, (edge, slots), 1)
    head_pick = (head_col == head_row + padding - least_pad).astype(jnp.float32).astype(jnp.bfloat16)
    query_live = lax.broadcasted_iota(jnp.int32, (rows_dev, head_dim), 0) < owned_count

    if n_units:
        from_diagonal(n_units - 1)
        from_sibling(n_units - 2)
        from_sibling(n_units - 1)
        total[...] += product(shards[n_units - 2]) + product(shards[n_units - 1])
    projected = total[...].astype(jnp.bfloat16)

    own_rows = pl.ds(2 * edge, slots)
    cand[own_rows, :] = projected
    tail = cand.at[pl.ds(rows_dev - edge, edge), :]
    send(lambda: tail, lambda: cand.at[pl.ds(0, edge), :], edge_send.at[0], edge_recv.at[0], {"sp": later})
    head[...] = jnp.dot(head_pick, projected, preferred_element_type=jnp.float32).astype(jnp.bfloat16)
    send(lambda: head, lambda: cand.at[pl.ds(edge, edge), :], edge_send.at[1], edge_recv.at[1], {"sp": prior})
    sent_edges = [copy for copy, _ in started[-2:]]
    del started[-2:]
    for j in range(n_units):
        started.extend(piece_copies(j))
    for copy, when in started:
        if when is None:
            copy().wait_send()
        else:
            pl.when(when)(lambda: copy().wait_send())
    arrived(cand.at[pl.ds(0, edge), :], edge_send.at[0], edge_recv.at[0], {"sp": later})
    arrived(cand.at[pl.ds(edge, edge), :], edge_send.at[1], edge_recv.at[1], {"sp": prior})

    qkv = jnp.dot(pick, cand[...], preferred_element_type=jnp.float32).astype(jnp.bfloat16)
    query, keys, values = qkv[:, :head_dim], qkv[:, head_dim : 2 * head_dim], qkv[:, 2 * head_dim :]
    scores = lax.dot_general(
        query, keys, (((1,), (1,)), ((), ())), preferred_element_type=jnp.float32
    ) * (1.0 / math.sqrt(head_dim))
    masked = jnp.where(allowed, scores, -1e30)
    peak = jnp.max(masked, axis=1, keepdims=True)
    exponent = jnp.where(allowed, jnp.exp(masked - peak), 0.0)
    probs = (exponent / jnp.sum(exponent, axis=1, keepdims=True)).astype(jnp.bfloat16)
    result = jnp.dot(probs, values, preferred_element_type=jnp.float32)
    out_ref[0] = jnp.where(query_live, result, 0.0).astype(out_ref.dtype)
    sent_edges[0]().wait_send()
    sent_edges[1]().wait_send()


def solution(mesh):
    n_sp, n_dp = mesh.shape["sp"], mesh.shape["dp"]

    def step(hidden, pad_counts, doc_lengths, range_shift, qkv_weight):
        rows_dev, width = hidden.shape[1:]
        depth, columns = qkv_weight.shape
        shares = share_count(n_sp // 2, depth // PARTS)
        edge, slots = rows_dev // 8, rows_dev - rows_dev // 4
        others = max(n_dp - 1, 1) * PARTS
        dma = pltpu.SemaphoreType.DMA
        return pl.pallas_call(
            functools.partial(kernel, n_sp, n_dp, shares),
            out_shape=jax.ShapeDtypeStruct((1, rows_dev, columns // 3), hidden.dtype),
            in_specs=[
                pl.BlockSpec(memory_space=pltpu.HBM),
            ]
            * 5,
            out_specs=pl.BlockSpec(memory_space=pltpu.VMEM),
            scratch_shapes=[
                pltpu.SMEM(pad_counts.shape, jnp.int32),
                pltpu.VMEM(doc_lengths.shape, jnp.int32),
                pltpu.SMEM(range_shift.shape, jnp.int32),
                pltpu.VMEM((slots, width), hidden.dtype),
                pltpu.VMEM((n_dp * PARTS, depth // PARTS, columns), qkv_weight.dtype),
                pltpu.VMEM((slots, columns), jnp.float32),
                pltpu.VMEM((n_sp, 8, 128), jnp.int32),
                pltpu.VMEM((rows_dev, columns), hidden.dtype),
                pltpu.VMEM((edge, columns), hidden.dtype),
                dma((5 + PARTS,)),
                dma(((n_dp + 2) * PARTS,)),
                dma((n_dp * PARTS,)),
                dma((others, 2)),
                dma((others, 2)),
                dma((others, 2)),
                dma((others, 2)),
                dma((others, shares)),
                dma((others, shares)),
                dma((n_sp - 1,)),
                dma((n_sp - 1,)),
                dma((2,)),
                dma((2,)),
            ],
            compiler_params=pltpu.CompilerParams(
                collective_id=0, has_side_effects=True, vmem_limit_bytes=63 * 1024 * 1024
            ),
            cost_estimate=pl.CostEstimate(
                flops=2 * slots * width * columns,
                bytes_accessed=2 * width * (rows_dev + columns),
                transcendentals=rows_dev * rows_dev,
            ),
        )(hidden, pad_counts, doc_lengths, range_shift, qkv_weight)

    in_specs = (P("dp", "sp", None), P("dp", "sp"), P("dp", None), P("dp", None), P("dp", None))
    return jax.shard_map(
        step, mesh=mesh, in_specs=in_specs, out_specs=P("dp", "sp", None), check_vma=False
    )
```
